256 devices in a mesh: gz: 8 (over z), gy: 8 (over x, y_hi), gx: 4 (over y_lo, core).
Axes of the slice: x: 4, y: 4 (y_hi: 2, y_lo: 2; y = y_hi * 2 + y_lo), z: 8, core: 2. Of those that a mesh axis runs over, the one named last changes fastest.
Arguments:
- recorded: bfloat16 [6, 3072, 2, 8, 512], P(None, ('gz', 'gy'), None, None, 'gx'), may hold values from 0.19921875 to 2
- tile_place: int32 [6, 3072], replicated, may hold values from 0 to 1023, as said below
- psf: float32 [6, 3, 31], replicated, may hold values from 0.009 to 1
- estimate: float32 [128, 128, 512], P('gz', 'gy', 'gx'), may hold values from 0.34 to 2.81
Outputs:
- restored: float32 [128, 128, 512], P('gz', 'gy', 'gx')
The draws below stay inside these ranges and needn't reach their ends.
Inputs may be any that keep to these rules, and one draw needn't show every extreme that they name: `tile_place`: tile j belongs to index j // 48 of gz+gy (gz slowest). For each view, the 48 tiles of one index name any block at most 2 times, and one block of each view is named exactly 2 times by the tiles of every index. Positions are below 16.
All inputs are finite; a program needn't handle non-finite values.
Results may differ from the reference program's by a relative error of at most 0.0009.
Values may be sent and summed in bfloat16 or wider, within the bound.
No kernel may reach another device: no remote copies, remote signals or barrier semaphores. Data moves between devices by JAX's collectives and lax.ppermute only.
A program may use at most 128 MiB of HBM per device.

```python
import jax
import jax.numpy as jnp
from jax import lax

VIEWS = 6
TAPS = 31
TZ = 2
TY = 8
BZ = 16
BY = 16
BX = 128
SLOTS = 48
ITERS = 1
ROUTE = 64
CAP = 2
TILES = 3072
POS = 16
NZ = 128
NY = 128
NX = 512
N_GY = 8


def draw_tile_place(key, part):
    key = jax.random.fold_in(key, 7)
    view_keys = jax.random.split(key, VIEWS)

    def one_view(view_key):
        hot_key, rest_key = jax.random.split(view_key)
        hottest = jax.random.randint(hot_key, (), 0, ROUTE)
        source_keys = jax.random.split(rest_key, ROUTE)

        def one_source(source_key):
            subkeys = jax.random.split(source_key, 4)
            elsewhere = (hottest + 1 + jax.random.permutation(subkeys[0], ROUTE - 1)) % ROUTE
            reserve = jax.random.permutation(subkeys[1], jnp.tile(elsewhere, CAP))
            chosen = jnp.concatenate([jnp.full((CAP,), hottest, jnp.int32), reserve[:SLOTS - CAP].astype(jnp.int32)])
            chosen = jax.random.permutation(subkeys[2], chosen)
            spot_index = jax.random.randint(subkeys[3], (SLOTS,), 0, POS)
            return chosen * POS + spot_index
        return jax.vmap(one_source)(source_keys).reshape(ROUTE * SLOTS)
    return jax.vmap(one_view)(view_keys).astype(jnp.int32)


def draw_psf(key, part):
    key = jax.random.fold_in(key, 11)
    strong_key, weak_key = jax.random.split(key)
    shape = (VIEWS, 3, TAPS)
    strong = jnp.exp(jax.random.uniform(strong_key, shape, jnp.float32, jnp.log(0.3), 0.0))
    weak = jnp.exp(jax.random.uniform(weak_key, shape, jnp.float32, jnp.log(0.0101), jnp.log(0.08)))
    odd_tap = jnp.arange(TAPS) % 2 == 1
    return jnp.where(odd_tap[None, None, :], strong, weak).astype(jnp.float32)


def draw_estimate(key, part):
    key = jax.random.fold_in(key, 13)
    period_key, phase_key, factor_key = jax.random.split(key, 3)
    periods = jnp.exp(jax.random.uniform(period_key, (3,), jnp.float32, jnp.log(40.0), jnp.log(120.0)))
    phases = jax.random.uniform(phase_key, (2,), jnp.float32, 0.0, 2.0 * jnp.pi)
    depth = jnp.arange(NZ)[:, None, None]
    rows = jnp.arange(NY)[None, :, None]
    columns = jnp.arange(NX)[None, None, :]
    parity = ((depth + rows + columns) % 2).astype(jnp.float32)
    signed = 1.0 - 2.0 * parity
    wave = 0.6 * jnp.cos(2.0 * jnp.pi * columns.astype(jnp.float32) / periods[0] + phases[0])
    wave = wave + 0.4 * jnp.cos(2.0 * jnp.pi * (rows.astype(jnp.float32) / periods[1] + depth.astype(jnp.float32) / periods[2]) + phases[1])
    base = 1.25 + 0.7 * signed * wave
    factor = jax.random.uniform(factor_key, (NZ, NY, NX), jnp.float32, 0.7, 1.4)
    return (base * factor).astype(jnp.float32)


def level_of(rng, dims, cuts, least, top_value):
    loudness = 1.0
    for dim, parts in cuts:
        steps = jax.random.uniform(jax.random.fold_in(jax.random.fold_in(rng, 6), dim), (parts,), jnp.float32, least / len(cuts), top_value / len(cuts))
        loudness = loudness * jnp.repeat(jnp.exp(steps), dims[dim] // parts).reshape((-1,) + (1,) * (len(dims) - 1 - dim))
    return loudness


def setup_inputs(seed: int = 0) -> dict:
    keys = jax.random.split(jax.random.key(seed), 5)
    recorded = jnp.clip(0.19921875 + 1.8007812 * jax.random.uniform(keys[0], (VIEWS, TILES, TZ, TY, NX), jnp.float32) ** level_of(keys[0], (VIEWS, TILES, TZ, TY, NX), ((1, 64), (4, 4)), -0.2, 0.2), 0.19921875, 2.0).astype(jnp.bfloat16)
    tile_place = draw_tile_place(jax.random.fold_in(keys[4], 71), 0)
    psf = draw_psf(jax.random.fold_in(keys[4], 71), 0)
    estimate = draw_estimate(jax.random.fold_in(keys[4], 71), 0)
    return dict(recorded=recorded, tile_place=tile_place, psf=psf, estimate=estimate)


background_level = 0.1


def banded(kernel, length):
    radius = (TAPS - 1) // 2
    offset = jnp.arange(length + 2 * radius)[:, None] - jnp.arange(length)[None, :]
    table = (offset[:, :, None] == jnp.arange(TAPS)[None, None, :]).astype(kernel.dtype)
    return jnp.einsum('aim,m->ai', table, kernel, precision=lax.Precision.HIGHEST)


def convolve_axis(volume, kernel, axis_index, block):
    radius = (TAPS - 1) // 2
    moved = jnp.moveaxis(volume, axis_index, -1)
    length = moved.shape[-1]
    padded = jnp.pad(moved, [(0, 0)] * (moved.ndim - 1) + [(radius, radius)])
    window = (jnp.arange(length // block)[:, None] * block + jnp.arange(block + 2 * radius)[None, :]).astype(jnp.int32)
    pieces = padded[..., window]
    result = jnp.einsum('...sa,ai->...si', pieces, banded(kernel, block), precision=lax.Precision.HIGHEST)
    result = result.reshape(moved.shape)
    return jnp.moveaxis(result, -1, axis_index)


def blur(volume, kernel_set):
    result = convolve_axis(volume, kernel_set[0], 0, BZ)
    result = convolve_axis(result, kernel_set[1], 1, BY)
    return convolve_axis(result, kernel_set[2], 2, BX)


def place_view(bundle):
    tiles, places = bundle
    per_row = BY // TY
    owner = places // POS
    slot_pos = places % POS
    z_start = (owner // N_GY) * BZ + (slot_pos // per_row) * TZ
    y_start = (owner % N_GY) * BY + (slot_pos % per_row) * TY
    z_index = (z_start[:, None, None] + jnp.arange(TZ)[None, :, None]).astype(jnp.int32)
    y_index = (y_start[:, None, None] + jnp.arange(TY)[None, None, :]).astype(jnp.int32)
    return jnp.zeros((NZ, NY, NX), jnp.float32).at[z_index, y_index].add(tiles.astype(jnp.float32))


def reference(recorded, tile_place, psf, estimate):
    kernels = psf / jnp.sum(psf, axis=-1, keepdims=True)
    joined = lax.map(place_view, (recorded, tile_place))
    for iteration in range(ITERS):
        current = estimate

        def accumulate(total, bundle):
            observed, kernel_set = bundle
            blurred = blur(current, kernel_set) + background_level
            ratio_field = observed / blurred
            return total + blur(ratio_field, kernel_set[:, ::-1]), None

        total, ignored = lax.scan(accumulate, jnp.zeros_like(estimate), (joined, kernels))
        estimate = estimate * total / VIEWS
    return estimate
```

```python
import jax
import jax.numpy as jnp
from jax import lax
from jax.sharding import PartitionSpec as P

background_level = 0.1
highest = lax.Precision.HIGHEST


def shift(value, axis, step):
    devices = lax.axis_size(axis)
    pairs = [(i, i + step) for i in range(devices) if 0 <= i + step < devices]
    return lax.ppermute(value, axis, pairs)


def taps_table(kernel_set, offset):
    taps = kernel_set.shape[-1]
    table = (offset[:, :, None] == jnp.arange(taps)[None, None, :]).astype(jnp.float32)
    return jnp.einsum("eim,vm->vei", table, kernel_set, precision=highest)


def pack_columns(value, groups):
    rows = value.shape[0] // groups
    return jnp.concatenate([value[g * rows : (g + 1) * rows] for g in range(groups)], axis=1)


def unpack_columns(value, groups):
    width = value.shape[1] // groups
    return jnp.concatenate([value[:, g * width : (g + 1) * width] for g in range(groups)], axis=0)


def route_tiles(recorded, tile_place, positions):
    view_count, slot_count = recorded.shape[:2]
    tile_width = recorded.shape[2] * recorded.shape[3] * recorded.shape[4]
    route_count = lax.axis_size(("gz", "gy"))
    my_index = lax.axis_index(("gz", "gy"))
    capacity = max(2, 2 * slot_count // route_count)
    placed = tile_place.reshape(view_count, route_count, slot_count)
    destination = placed // positions
    position = placed % positions
    matching = destination[..., :, None] == destination[..., None, :]
    earlier = jnp.arange(slot_count)[None, :] < jnp.arange(slot_count)[:, None]
    ranking = jnp.sum(matching & earlier, axis=-1)
    my_dest = lax.dynamic_index_in_dim(destination, my_index, 1, keepdims=False)
    my_rank = lax.dynamic_index_in_dim(ranking, my_index, 1, keepdims=False)
    target = my_dest * capacity + my_rank
    picker = (jnp.arange(route_count * capacity)[None, :, None] == target[:, None, :]).astype(
        jnp.bfloat16
    )
    outgoing = jnp.einsum(
        "vbs,vsk->vbk",
        picker,
        recorded.reshape(view_count, slot_count, tile_width),
        preferred_element_type=jnp.float32,
    ).astype(jnp.bfloat16)
    arrived = lax.all_to_all(outgoing, ("gz", "gy"), split_axis=1, concat_axis=1, tiled=True)
    owned_here = destination == my_index
    at_position = ((position[..., None] == jnp.arange(positions)) & owned_here[..., None]).astype(
        jnp.float32
    )
    at_rank = (ranking[..., None] == jnp.arange(capacity)).astype(jnp.float32)
    placer = (
        jnp.einsum("vrsp,vrsc->vprc", at_position, at_rank)
        .reshape(view_count, positions, route_count * capacity)
        .astype(jnp.bfloat16)
    )
    return jnp.einsum("vpb,vbk->vpk", placer, arrived, preferred_element_type=jnp.float32)


def on_device(recorded, tile_place, psf, estimate):
    view_count = recorded.shape[0]
    tile_depth, tile_rows = recorded.shape[2:4]
    depth, rows, cols = estimate.shape
    per_row = rows // tile_rows
    positions = depth // tile_depth * per_row
    area = depth * rows
    radius = (psf.shape[2] - 1) // 2
    side = 16
    tall, wide = depth + 2 * side, rows + 2 * side
    joined = route_tiles(recorded, tile_place, positions).reshape(view_count, area, cols)

    kernels = psf / jnp.sum(psf, axis=-1, keepdims=True)
    line = jnp.arange(area)
    place, inside = line // (tile_depth * tile_rows), line % (tile_depth * tile_rows)
    line_depth = place // per_row * tile_depth + inside // tile_rows
    line_row = place % per_row * tile_rows + inside % tile_rows
    reach = radius - side
    depth_taps = taps_table(kernels[:, 0], jnp.arange(tall)[:, None] - line_depth[None, :] + reach)
    row_taps = taps_table(kernels[:, 1], jnp.arange(wide)[:, None] - line_row[None, :] + reach)
    depth_taps = depth_taps.transpose(1, 0, 2).reshape(tall, view_count * area)
    row_taps = row_taps.transpose(1, 0, 2).reshape(wide, view_count * area)
    sheet = (depth_taps[:, None, :] * row_taps[None, :, :]).astype(jnp.bfloat16)
    sheet = sheet.reshape(tall * wide, view_count * area)
    column = jnp.concatenate(
        [jnp.arange(cols), jnp.arange(-side, 0), jnp.arange(cols, cols + side)]
    )
    col_taps = taps_table(
        kernels[:, 2], column[:, None] - jnp.arange(cols)[None, :] + radius
    ).astype(jnp.bfloat16)

    own = estimate.astype(jnp.bfloat16)
    own = jnp.concatenate([shift(own, "gy", 1), own, shift(own, "gy", -1)], axis=1)
    own = jnp.concatenate([shift(own, "gz", 1), own, shift(own, "gz", -1)], axis=0)
    own = own.reshape(tall * wide, cols)
    groups = cols // side
    before = unpack_columns(shift(pack_columns(own[:, cols - side :], groups), "gx", 1), groups)
    after = unpack_columns(shift(pack_columns(own[:, :side], groups), "gx", -1), groups)
    field = jnp.concatenate([own, before, after], axis=1)
    swept = lax.dot_general(
        sheet, field, (((0,), (0,)), ((), ())), preferred_element_type=jnp.float32
    )
    swept = swept.astype(jnp.bfloat16).reshape(view_count, area, -1)
    blurred = jnp.einsum("vac,vck->vak", swept, col_taps, preferred_element_type=jnp.float32)
    ratio = (joined / (blurred + background_level)).astype(jnp.bfloat16)

    spread = jnp.einsum("vak,vck->vac", ratio, col_taps, preferred_element_type=jnp.float32)
    spread = spread.astype(jnp.bfloat16).reshape(view_count * area, -1)
    total = jnp.dot(sheet, spread, preferred_element_type=jnp.float32)
    leftward = pack_columns(total[:, cols : cols + side], groups).astype(jnp.bfloat16)
    rightward = pack_columns(total[:, cols + side :], groups).astype(jnp.bfloat16)
    from_right = unpack_columns(shift(leftward, "gx", -1), groups).astype(jnp.float32)
    from_left = unpack_columns(shift(rightward, "gx", 1), groups).astype(jnp.float32)
    edge = jnp.zeros((tall * wide, cols - 2 * side), jnp.float32)
    total = total[:, :cols] + jnp.concatenate([from_left, edge, from_right], axis=1)
    total = total.reshape(tall, wide, cols)
    upper = shift(total[:side].astype(jnp.bfloat16), "gz", -1)
    lower = shift(total[tall - side :].astype(jnp.bfloat16), "gz", 1)
    total = total[side : side + depth] + upper.astype(jnp.float32) + lower.astype(jnp.float32)
    upper = shift(total[:, :side].astype(jnp.bfloat16), "gy", -1)
    lower = shift(total[:, wide - side :].astype(jnp.bfloat16), "gy", 1)
    total = total[:, side : side + rows] + upper.astype(jnp.float32) + lower.astype(jnp.float32)
    return estimate * total / view_count


def solution(mesh):
    placed = (P(None, ("gz", "gy"), None, None, "gx"), P(), P(), P("gz", "gy", "gx"))
    return jax.shard_map(
        on_device, mesh=mesh, in_specs=placed, out_specs=P("gz", "gy", "gx"), check_vma=False
    )
```

```python
import jax
import jax.numpy as jnp
from jax import lax
from jax.experimental import pallas as pl
from jax.experimental.pallas import tpu as pltpu
from jax.sharding import PartitionSpec as P

background_level = 0.1
highest = lax.Precision.HIGHEST
capacity = 2


def shift(value, axis, step):
    devices = lax.axis_size(axis)
    pairs = [(i, i + step) for i in range(devices) if 0 <= i + step < devices]
    return lax.ppermute(value, axis, pairs)


def taps_table(kernel_set, offset):
    taps = kernel_set.shape[-1]
    table = (offset[:, :, None] == jnp.arange(taps)[None, None, :]).astype(jnp.float32)
    return jnp.einsum("eim,vm->vei", table, kernel_set, precision=highest)


def pack_columns(value, groups):
    rows = value.shape[0] // groups
    return jnp.concatenate([value[g * rows : (g + 1) * rows] for g in range(groups)], axis=1)


def unpack_columns(value, groups):
    width = value.shape[1] // groups
    return jnp.concatenate([value[:, g * width : (g + 1) * width] for g in range(groups)], axis=0)


def group_places(tile_place, positions):
    view_count = tile_place.shape[0]
    gz_count, gy_count = lax.axis_size("gz"), lax.axis_size("gy")
    my_gz, my_gy = lax.axis_index("gz"), lax.axis_index("gy")
    placed = tile_place.reshape(view_count, gz_count, gy_count, -1)
    placed = lax.dynamic_index_in_dim(placed, my_gz, 1, keepdims=False)
    slot_count = placed.shape[-1]
    destination = placed // positions
    position = placed % positions
    matching = destination[..., :, None] == destination[..., None, :]
    earlier = jnp.arange(slot_count)[None, :] < jnp.arange(slot_count)[:, None]
    ranking = jnp.sum(matching & earlier, axis=-1)
    lane = destination // gy_count * capacity + ranking
    dest_gy = destination % gy_count
    lanes = gz_count * capacity
    own_lane = lax.dynamic_index_in_dim(lane, my_gy, 1, keepdims=False)
    own_dest = lax.dynamic_index_in_dim(dest_gy, my_gy, 1, keepdims=False)
    wanted = jnp.arange(gy_count * lanes)[None, :, None]
    chosen = wanted == (own_dest * lanes + own_lane)[:, None, :]
    source = jnp.sum(chosen * jnp.arange(slot_count)[None, None, :], axis=-1)
    here = (dest_gy == my_gy)[:, :, None, :] & (jnp.arange(lanes)[:, None] == lane[:, :, None, :])
    cell = jnp.sum(here * (position - positions)[:, :, None, :], axis=-1) + positions
    return source.astype(jnp.int32), cell.astype(jnp.int32)


def pack_kernel(source, tiles, outgoing):
    partners, views, lanes = outgoing.shape[:3]
    for view in range(views):
        for partner in range(partners):
            for lane in range(lanes):
                index = source[view, partner * lanes + lane]
                outgoing[partner, view, lane] = tiles[view, index]


def join_kernel(cell, arrived, partial, total):
    partners, views = arrived.shape[:2]
    blocks, _, positions = partial.shape[:3]

    def one_view(view, carry):
        for block in range(blocks):
            total[...] = jnp.zeros_like(total)
            for partner in range(partners):
                for rank in range(capacity):
                    lane = block * capacity + rank
                    index = cell[view, partner, lane]
                    total[index] += arrived[partner, view, lane].astype(jnp.float32)
            partial[block, view] = total[:positions].astype(partial.dtype)
        return carry

    lax.fori_loop(0, views, one_view, 0)


def route_tiles(recorded, tile_place, positions):
    view_count, slot_count = recorded.shape[:2]
    height = recorded.shape[2] * recorded.shape[3]
    cols = recorded.shape[4]
    gz_count, gy_count = lax.axis_size("gz"), lax.axis_size("gy")
    source, cell = group_places(tile_place, positions)
    smem = pl.BlockSpec(memory_space=pltpu.SMEM)
    vmem = pl.BlockSpec(memory_space=pltpu.VMEM)
    lanes = gz_count * capacity
    outgoing = pl.pallas_call(
        pack_kernel,
        out_shape=jax.ShapeDtypeStruct((gy_count, view_count, lanes, height, cols), recorded.dtype),
        in_specs=[smem, vmem],
        out_specs=vmem,
        compiler_params=pltpu.CompilerParams(vmem_limit_bytes=32 << 20),
        name="pack",
    )(source, recorded.reshape(view_count, slot_count, height, cols))
    arrived = lax.all_to_all(outgoing, "gy", split_axis=0, concat_axis=0, tiled=True)
    partial = pl.pallas_call(
        join_kernel,
        out_shape=jax.ShapeDtypeStruct(
            (gz_count, view_count, positions, height, cols), recorded.dtype
        ),
        in_specs=[smem, vmem],
        out_specs=vmem,
        scratch_shapes=[pltpu.VMEM((positions + 1, height, cols), jnp.float32)],
        compiler_params=pltpu.CompilerParams(vmem_limit_bytes=32 << 20),
        name="join",
    )(cell, arrived)
    partial = partial.reshape(gz_count, view_count * positions * height, cols)
    joined = lax.psum_scatter(partial, "gz", scatter_dimension=0, tiled=False)
    return joined.astype(jnp.float32)


def on_device(recorded, tile_place, psf, estimate):
    view_count = recorded.shape[0]
    tile_depth, tile_rows = recorded.shape[2:4]
    depth, rows, cols = estimate.shape
    per_row = rows // tile_rows
    positions = depth // tile_depth * per_row
    area = depth * rows
    radius = (psf.shape[2] - 1) // 2
    side = 16
    tall, wide = depth + 2 * side, rows + 2 * side
    joined = route_tiles(recorded, tile_place, positions).reshape(view_count, area, cols)

    kernels = psf / jnp.sum(psf, axis=-1, keepdims=True)
    line = jnp.arange(area)
    place, inside = line // (tile_depth * tile_rows), line % (tile_depth * tile_rows)
    line_depth = place // per_row * tile_depth + inside // tile_rows
    line_row = place % per_row * tile_rows + inside % tile_rows
    reach = radius - side
    depth_taps = taps_table(kernels[:, 0], jnp.arange(tall)[:, None] - line_depth[None, :] + reach)
    row_taps = taps_table(kernels[:, 1], jnp.arange(wide)[:, None] - line_row[None, :] + reach)
    depth_taps = depth_taps.transpose(1, 0, 2).reshape(tall, view_count * area)
    row_taps = row_taps.transpose(1, 0, 2).reshape(wide, view_count * area)
    sheet = (depth_taps[:, None, :] * row_taps[None, :, :]).astype(jnp.bfloat16)
    sheet = sheet.reshape(tall * wide, view_count * area)
    column = jnp.concatenate(
        [jnp.arange(cols), jnp.arange(-side, 0), jnp.arange(cols, cols + side)]
    )
    col_taps = taps_table(
        kernels[:, 2], column[:, None] - jnp.arange(cols)[None, :] + radius
    ).astype(jnp.bfloat16)

    own = estimate.astype(jnp.bfloat16)
    own = jnp.concatenate([shift(own, "gy", 1), own, shift(own, "gy", -1)], axis=1)
    own = jnp.concatenate([shift(own, "gz", 1), own, shift(own, "gz", -1)], axis=0)
    own = own.reshape(tall * wide, cols)
    groups = cols // side
    before = unpack_columns(shift(pack_columns(own[:, cols - side :], groups), "gx", 1), groups)
    after = unpack_columns(shift(pack_columns(own[:, :side], groups), "gx", -1), groups)
    field = jnp.concatenate([own, before, after], axis=1)
    swept = lax.dot_general(
        sheet, field, (((0,), (0,)), ((), ())), preferred_element_type=jnp.float32
    )
    swept = swept.astype(jnp.bfloat16).reshape(view_count, area, -1)
    blurred = jnp.einsum("vac,vck->vak", swept, col_taps, preferred_element_type=jnp.float32)
    ratio = (joined / (blurred + background_level)).astype(jnp.bfloat16)

    spread = jnp.einsum("vak,vck->vac", ratio, col_taps, preferred_element_type=jnp.float32)
    spread = spread.astype(jnp.bfloat16).reshape(view_count * area, -1)
    total = jnp.dot(sheet, spread, preferred_element_type=jnp.float32)
    leftward = pack_columns(total[:, cols : cols + side], groups).astype(jnp.bfloat16)
    rightward = pack_columns(total[:, cols + side :], groups).astype(jnp.bfloat16)
    from_right = unpack_columns(shift(leftward, "gx", -1), groups).astype(jnp.float32)
    from_left = unpack_columns(shift(rightward, "gx", 1), groups).astype(jnp.float32)
    edge = jnp.zeros((tall * wide, cols - 2 * side), jnp.float32)
    total = total[:, :cols] + jnp.concatenate([from_left, edge, from_right], axis=1)
    total = total.reshape(tall, wide, cols)
    upper = shift(total[:side].astype(jnp.bfloat16), "gz", -1)
    lower = shift(total[tall - side :].astype(jnp.bfloat16), "gz", 1)
    total = total[side : side + depth] + upper.astype(jnp.float32) + lower.astype(jnp.float32)
    upper = shift(total[:, :side], "gy", -1)
    lower = shift(total[:, wide - side :], "gy", 1)
    total = total[:, side : side + rows] + upper + lower
    return estimate * total / view_count


def solution(mesh):
    placed = (P(None, ("gz", "gy"), None, None, "gx"), P(), P(), P("gz", "gy", "gx"))
    return jax.shard_map(
        on_device, mesh=mesh, in_specs=placed, out_specs=P("gz", "gy", "gx"), check_vma=False
    )
```

```python
import jax
import jax.numpy as jnp
from jax import lax
from jax.experimental import pallas as pl
from jax.experimental.pallas import tpu as pltpu
from jax.sharding import PartitionSpec as P

background_level = 0.1
highest = lax.Precision.HIGHEST
capacity = 2


def shift(value, axis, step):
    devices = lax.axis_size(axis)
    pairs = [(i, i + step) for i in range(devices) if 0 <= i + step < devices]
    return lax.ppermute(value, axis, pairs)


def taps_table(kernel_set, offset):
    taps = kernel_set.shape[-1]
    table = (offset[:, :, None] == jnp.arange(taps)[None, None, :]).astype(jnp.float32)
    return jnp.einsum("eim,vm->vei", table, kernel_set, precision=highest)


def pack_columns(value, groups):
    rows = value.shape[0] // groups
    return jnp.concatenate([value[g * rows : (g + 1) * rows] for g in range(groups)], axis=1)


def unpack_columns(value, groups):
    width = value.shape[1] // groups
    return jnp.concatenate([value[:, g * width : (g + 1) * width] for g in range(groups)], axis=0)


def group_places(tile_place, positions):
    view_count = tile_place.shape[0]
    gz_count, gy_count = lax.axis_size("gz"), lax.axis_size("gy")
    my_gz, my_gy = lax.axis_index("gz"), lax.axis_index("gy")
    placed = tile_place.reshape(view_count, gz_count, gy_count, -1)
    placed = lax.dynamic_index_in_dim(placed, my_gz, 1, keepdims=False)
    slot_count = placed.shape[-1]
    destination = placed // positions
    position = placed % positions
    matching = destination[..., :, None] == destination[..., None, :]
    earlier = jnp.arange(slot_count)[None, :] < jnp.arange(slot_count)[:, None]
    ranking = jnp.sum(matching & earlier, axis=-1)
    ahead = (destination // gy_count - my_gz) % gz_count
    lane = ahead * capacity + ranking
    dest_gy = destination % gy_count
    lanes = gz_count * capacity
    own_lane = lax.dynamic_index_in_dim(lane, my_gy, 1, keepdims=False)
    own_dest = lax.dynamic_index_in_dim(dest_gy, my_gy, 1, keepdims=False)
    wanted = jnp.arange(gy_count * lanes)[None, :, None]
    chosen = wanted == (own_dest * lanes + own_lane)[:, None, :]
    source = jnp.sum(chosen * jnp.arange(slot_count)[None, None, :], axis=-1)
    here = (dest_gy == my_gy)[:, :, None, :] & (jnp.arange(lanes)[:, None] == lane[:, :, None, :])
    cell = jnp.sum(here * (position - positions)[:, :, None, :], axis=-1) + positions
    return source.astype(jnp.int32), cell.astype(jnp.int32)


def pack_kernel(source, tiles, outgoing):
    partners, views, lanes = outgoing.shape[:3]
    for view in range(views):
        for partner in range(partners):
            for lane in range(lanes):
                index = source[view, partner * lanes + lane]
                outgoing[partner, view, lane] = tiles[view, index]


def join_kernel(cell, arrived, partial, total):
    partners, views = arrived.shape[:2]
    blocks, _, positions = partial.shape[:3]

    def one_view(view, carry):
        for block in range(blocks):
            total[...] = jnp.zeros_like(total)
            for partner in range(partners):
                for rank in range(capacity):
                    lane = block * capacity + rank
                    index = cell[view, partner, lane]
                    total[index] += arrived[partner, view, lane].astype(jnp.float32)
            partial[block, view] = total[:positions].astype(partial.dtype)
        return carry

    lax.fori_loop(0, views, one_view, 0)


def add_rounded(left, right):
    return (left.astype(jnp.float32) + right.astype(jnp.float32)).astype(left.dtype)


def ring_sum(partial):
    devices, rows = partial.shape[:2]
    half, middle = devices // 2, rows // 2
    up = [(i, (i + 1) % devices) for i in range(devices)]
    down = [(j, i) for i, j in up]
    from_below = lax.ppermute(partial[half, :middle], "gz", up)
    from_above = lax.ppermute(partial[half, middle:], "gz", down)
    for ahead in range(half - 1, 0, -1):
        upward, downward = partial[ahead], partial[devices - ahead]
        if ahead == half - 1:
            upward = jnp.concatenate([add_rounded(upward[:middle], from_below), upward[middle:]])
            downward = jnp.concatenate(
                [downward[:middle], add_rounded(downward[middle:], from_above)]
            )
        else:
            upward = add_rounded(upward, from_below)
            downward = add_rounded(downward, from_above)
        from_below = lax.ppermute(upward, "gz", up)
        from_above = lax.ppermute(downward, "gz", down)
    return (
        partial[0].astype(jnp.float32)
        + from_below.astype(jnp.float32)
        + from_above.astype(jnp.float32)
    )


def route_tiles(tiles, source, cell, positions):
    view_count, _, height, cols = tiles.shape
    gz_count, gy_count = lax.axis_size("gz"), lax.axis_size("gy")
    smem = pl.BlockSpec(memory_space=pltpu.SMEM)
    vmem = pl.BlockSpec(memory_space=pltpu.VMEM)
    lanes = gz_count * capacity
    outgoing = pl.pallas_call(
        pack_kernel,
        out_shape=jax.ShapeDtypeStruct((gy_count, view_count, lanes, height, cols), tiles.dtype),
        in_specs=[smem, vmem],
        out_specs=vmem,
        compiler_params=pltpu.CompilerParams(vmem_limit_bytes=32 << 20),
        name="pack",
    )(source, tiles)
    arrived = lax.all_to_all(outgoing, "gy", split_axis=0, concat_axis=0, tiled=True)
    partial = pl.pallas_call(
        join_kernel,
        out_shape=jax.ShapeDtypeStruct(
            (gz_count, view_count, positions, height, cols), tiles.dtype
        ),
        in_specs=[smem, vmem],
        out_specs=vmem,
        scratch_shapes=[pltpu.VMEM((positions + 1, height, cols), jnp.float32)],
        compiler_params=pltpu.CompilerParams(vmem_limit_bytes=32 << 20),
        name="join",
    )(cell, arrived)
    return ring_sum(partial.reshape(gz_count, view_count * positions * height, cols))


def on_device(recorded, tile_place, psf, estimate):
    view_count = recorded.shape[0]
    tile_depth, tile_rows = recorded.shape[2:4]
    depth, rows, cols = estimate.shape
    per_row = rows // tile_rows
    positions = depth // tile_depth * per_row
    area = depth * rows
    radius = (psf.shape[2] - 1) // 2
    side = 16
    tall, wide = depth + 2 * side, rows + 2 * side
    tiles = recorded.reshape(view_count, -1, tile_depth * tile_rows, cols)
    source, cell = group_places(tile_place, positions)
    chunk = view_count // 2
    joined = [
        route_tiles(tiles[v : v + chunk], source[v : v + chunk], cell[v : v + chunk], positions)
        for v in range(0, view_count, chunk)
    ]
    joined = jnp.concatenate(joined).reshape(view_count, area, cols)

    kernels = psf / jnp.sum(psf, axis=-1, keepdims=True)
    line = jnp.arange(area)
    place, inside = line // (tile_depth * tile_rows), line % (tile_depth * tile_rows)
    line_depth = place // per_row * tile_depth + inside // tile_rows
    line_row = place % per_row * tile_rows + inside % tile_rows
    reach = radius - side
    depth_taps = taps_table(kernels[:, 0], jnp.arange(tall)[:, None] - line_depth[None, :] + reach)
    row_taps = taps_table(kernels[:, 1], jnp.arange(wide)[:, None] - line_row[None, :] + reach)
    depth_taps = depth_taps.transpose(1, 0, 2).reshape(tall, view_count * area)
    row_taps = row_taps.transpose(1, 0, 2).reshape(wide, view_count * area)
    sheet = (depth_taps[:, None, :] * row_taps[None, :, :]).astype(jnp.bfloat16)
    sheet = sheet.reshape(tall * wide, view_count * area)
    column = jnp.concatenate(
        [jnp.arange(cols), jnp.arange(-side, 0), jnp.arange(cols, cols + side)]
    )
    col_taps = taps_table(
        kernels[:, 2], column[:, None] - jnp.arange(cols)[None, :] + radius
    ).astype(jnp.bfloat16)

    own = estimate.astype(jnp.bfloat16)
    own = jnp.concatenate([shift(own, "gy", 1), own, shift(own, "gy", -1)], axis=1)
    own = jnp.concatenate([shift(own, "gz", 1), own, shift(own, "gz", -1)], axis=0)
    own = own.reshape(tall * wide, cols)
    groups = cols // side
    before = unpack_columns(shift(pack_columns(own[:, cols - side :], groups), "gx", 1), groups)
    after = unpack_columns(shift(pack_columns(own[:, :side], groups), "gx", -1), groups)
    field = jnp.concatenate([own, before, after], axis=1)
    swept = lax.dot_general(
        sheet, field, (((0,), (0,)), ((), ())), preferred_element_type=jnp.float32
    )
    swept = swept.astype(jnp.bfloat16).reshape(view_count, area, -1)
    blurred = jnp.einsum("vac,vck->vak", swept, col_taps, preferred_element_type=jnp.float32)
    ratio = (joined / (blurred + background_level)).astype(jnp.bfloat16)

    spread = jnp.einsum("vak,vck->vac", ratio, col_taps, preferred_element_type=jnp.float32)
    spread = spread.astype(jnp.bfloat16).reshape(view_count * area, -1)
    total = jnp.dot(sheet, spread, preferred_element_type=jnp.float32)
    leftward = pack_columns(total[:, cols : cols + side], groups).astype(jnp.bfloat16)
    rightward = pack_columns(total[:, cols + side :], groups).astype(jnp.bfloat16)
    from_right = unpack_columns(shift(leftward, "gx", -1), groups).astype(jnp.float32)
    from_left = unpack_columns(shift(rightward, "gx", 1), groups).astype(jnp.float32)
    edge = jnp.zeros((tall * wide, cols - 2 * side), jnp.float32)
    total = total[:, :cols] + jnp.concatenate([from_left, edge, from_right], axis=1)
    total = total.reshape(tall, wide, cols)
    upper = shift(total[:side].astype(jnp.bfloat16), "gz", -1)
    lower = shift(total[tall - side :].astype(jnp.bfloat16), "gz", 1)
    total = total[side : side + depth] + upper.astype(jnp.float32) + lower.astype(jnp.float32)
    upper = shift(total[:, :side], "gy", -1)
    lower = shift(total[:, wide - side :], "gy", 1)
    total = total[:, side : side + rows] + upper + lower
    return estimate * total / view_count


def solution(mesh):
    placed = (P(None, ("gz", "gy"), None, None, "gx"), P(), P(), P("gz", "gy", "gx"))
    return jax.shard_map(
        on_device, mesh=mesh, in_specs=placed, out_specs=P("gz", "gy", "gx"), check_vma=False
    )
```

```python
import functools

import jax
import jax.numpy as jnp
from jax import lax
from jax.experimental import pallas as pl
from jax.experimental.pallas import tpu as pltpu
from jax.sharding import PartitionSpec as P

background_level = 0.1
highest = lax.Precision.HIGHEST
capacity = 2
usual_slots = 56


def shift(value, axis, step):
    devices = lax.axis_size(axis)
    pairs = [(i, i + step) for i in range(devices) if 0 <= i + step < devices]
    return lax.ppermute(value, axis, pairs)


def taps_table(kernel_set, offset):
    taps = kernel_set.shape[-1]
    table = (offset[:, :, None] == jnp.arange(taps)[None, None, :]).astype(jnp.float32)
    return jnp.einsum("eim,vm->vei", table, kernel_set, precision=highest)


def pack_columns(value, groups):
    rows = value.shape[0] // groups
    return jnp.concatenate([value[g * rows : (g + 1) * rows] for g in range(groups)], axis=1)


def unpack_columns(value, groups):
    width = value.shape[1] // groups
    return jnp.concatenate([value[:, g * width : (g + 1) * width] for g in range(groups)], axis=0)


def slot_tables(tile_place, positions, chunks, usual):
    view_count = tile_place.shape[0]
    gz_count, gy_count = lax.axis_size("gz"), lax.axis_size("gy")
    my_gz, my_gy = lax.axis_index("gz"), lax.axis_index("gy")
    chunk = view_count // chunks
    placed = tile_place.reshape(view_count, gz_count, gy_count, -1)
    slot_count = placed.shape[-1]
    entries = view_count * slot_count
    group = lax.dynamic_index_in_dim(placed, my_gz, 1, keepdims=False)
    group = group.transpose(1, 0, 2).reshape(gy_count, entries)
    destination = group // positions
    dest_gy = destination % gy_count
    ahead = (destination // gy_count - my_gz) % gz_count
    view = jnp.arange(entries) // slot_count % chunk
    cell = (ahead * chunk + view) * positions + group % positions
    own_dest = lax.dynamic_index_in_dim(dest_gy, my_gy, 0, keepdims=True)
    sends = own_dest == jnp.arange(gy_count)[:, None]
    takes = dest_gy == my_gy
    number = jnp.broadcast_to(jnp.arange(entries)[None, :], takes.shape)
    chosen = jnp.stack([sends, takes])
    value = jnp.stack([number, cell])
    upto = (jnp.arange(entries)[:, None] <= jnp.arange(entries)[None, :]).astype(jnp.bfloat16)
    rank = jnp.dot(chosen.astype(jnp.bfloat16), upto, preferred_element_type=jnp.float32)
    rank = jnp.where(chosen, rank.astype(jnp.int32) - 1, -1)

    def table(first, lanes):
        hit = rank[..., None, :] == first + jnp.arange(lanes)[:, None]
        return jnp.sum(jnp.where(hit, value[..., None, :], 0), axis=-1).astype(jnp.int32)

    ends = [
        jnp.sum(takes[:, : c * chunk * slot_count], axis=-1).astype(jnp.int32)
        for c in range(chunks + 1)
    ]
    return table, jnp.stack(ends)


def most_slots(tile_place, positions):
    gy_count = lax.axis_size("gy")
    route_count = lax.axis_size(("gz", "gy"))
    dest_gy = (tile_place // positions) % gy_count
    dest_gy = dest_gy.reshape(tile_place.shape[0], route_count, 1, -1)
    return jnp.max(jnp.sum(dest_gy == jnp.arange(gy_count)[:, None], axis=(0, 3)))


def pack_kernel(source, tiles, outgoing):
    partners, lanes = outgoing.shape[:2]
    for partner in range(partners):
        for lane in range(lanes):
            outgoing[partner, lane] = tiles[source[partner, lane]]


def join_kernel(chunk, ends, cell, late_cell, arrived, late, *blocks_and_total):
    blocks, total = blocks_and_total[:-1], blocks_and_total[-1]
    partners, usual = arrived.shape[:2]
    step = 16

    def clear(index, carry):
        total[pl.ds(index * step, step)] = jnp.zeros((step,) + total.shape[1:], total.dtype)
        return carry

    lax.fori_loop(0, total.shape[0] // step, clear, 0)

    def add(cells, tiles, partner, lane):
        place = cells[partner, lane]
        total[place] = add_rounded(total[place], tiles[partner, lane])

    for partner in range(partners):
        first, last = ends[chunk, partner], ends[chunk + 1, partner]

        def add_usual(lane, carry):
            add(cell, arrived, partner, lane)
            return carry

        def add_late(lane, carry):
            add(late_cell, late, partner, lane - usual)
            return carry

        lax.fori_loop(jnp.minimum(first, usual), jnp.minimum(last, usual), add_usual, 0)
        lax.fori_loop(jnp.maximum(first, usual), jnp.maximum(last, usual), add_late, 0)
    start = 0
    for block in blocks:
        block[...] = total[start : start + block.shape[0]]
        start += block.shape[0]


smem = pl.BlockSpec(memory_space=pltpu.SMEM)
vmem = pl.BlockSpec(memory_space=pltpu.VMEM)


def pack(source, tiles):
    return pl.pallas_call(
        pack_kernel,
        out_shape=jax.ShapeDtypeStruct(source.shape + tiles.shape[1:], tiles.dtype),
        in_specs=[smem, vmem],
        out_specs=vmem,
        compiler_params=pltpu.CompilerParams(vmem_limit_bytes=32 << 20),
        name="pack",
    )(source, tiles)


def join(chunk, ends, cell, late_cell, arrived, late, devices, cells):
    tile = arrived.shape[2:]
    half = devices // 2
    sizes = [cells] * half + [cells // 2] * 2 + [cells] * (half - 1)
    return pl.pallas_call(
        functools.partial(join_kernel, chunk),
        out_shape=[jax.ShapeDtypeStruct((size,) + tile, arrived.dtype) for size in sizes],
        in_specs=[smem, smem, smem, vmem, vmem],
        out_specs=[vmem] * len(sizes),
        scratch_shapes=[pltpu.VMEM((devices * cells,) + tile, arrived.dtype)],
        compiler_params=pltpu.CompilerParams(vmem_limit_bytes=32 << 20),
        name="join",
    )(ends, cell, late_cell, arrived, late)


def exchange(value):
    return lax.all_to_all(value, "gy", split_axis=0, concat_axis=0, tiled=True)


def exchange_by_permutes(value):
    devices, me = lax.axis_size("gy"), lax.axis_index("gy")
    result = value
    for step in range(1, devices):
        part = lax.dynamic_index_in_dim(value, (me + step) % devices, 0)
        part = lax.ppermute(part, "gy", [(i, (i + step) % devices) for i in range(devices)])
        result = lax.dynamic_update_index_in_dim(result, part, (me - step) % devices, 0)
    return result


def add_rounded(left, right):
    return (left.astype(jnp.float32) + right.astype(jnp.float32)).astype(left.dtype)


def ring_sum(blocks):
    devices = len(blocks) - 1
    half = devices // 2
    up = [(i, (i + 1) % devices) for i in range(devices)]
    down = [(j, i) for i, j in up]
    middle = blocks[half].shape[0]
    from_below = lax.ppermute(blocks[half], "gz", up)
    from_above = lax.ppermute(blocks[half + 1], "gz", down)
    for ahead in range(half - 1, 0, -1):
        upward, downward = blocks[ahead], blocks[devices - ahead + 1]
        if ahead == half - 1:
            upward = jnp.concatenate([add_rounded(upward[:middle], from_below), upward[middle:]])
            downward = jnp.concatenate(
                [downward[:middle], add_rounded(downward[middle:], from_above)]
            )
        else:
            upward = add_rounded(upward, from_below)
            downward = add_rounded(downward, from_above)
        from_below = lax.ppermute(upward, "gz", up)
        from_above = lax.ppermute(downward, "gz", down)
    return (
        blocks[0].astype(jnp.float32)
        + from_below.astype(jnp.float32)
        + from_above.astype(jnp.float32)
    )


def on_device(recorded, tile_place, psf, estimate):
    view_count = recorded.shape[0]
    tile_depth, tile_rows = recorded.shape[2:4]
    depth, rows, cols = estimate.shape
    per_row = rows // tile_rows
    positions = depth // tile_depth * per_row
    area = depth * rows
    radius = (psf.shape[2] - 1) // 2
    side = 16
    tall, wide = depth + 2 * side, rows + 2 * side
    chunks = 2
    chunk = view_count // chunks
    gz_count, gy_count = lax.axis_size("gz"), lax.axis_size("gy")
    tiles = recorded.reshape(-1, tile_depth * tile_rows, cols)
    lanes = gz_count * capacity * view_count
    usual = min(usual_slots, lanes)
    table, ends = slot_tables(tile_place, positions, chunks, usual)
    usual_table = table(0, usual)
    outgoing, psf = lax.optimization_barrier((pack(usual_table[0], tiles), psf))
    arrived = exchange(outgoing)
    own = estimate.astype(jnp.bfloat16)

    kernels = psf / jnp.sum(psf, axis=-1, keepdims=True)
    line = jnp.arange(area)
    place, inside = line // (tile_depth * tile_rows), line % (tile_depth * tile_rows)
    line_depth = place // per_row * tile_depth + inside // tile_rows
    line_row = place % per_row * tile_rows + inside % tile_rows
    reach = radius - side
    depth_taps = taps_table(kernels[:, 0], jnp.arange(tall)[:, None] - line_depth[None, :] + reach)
    row_taps = taps_table(kernels[:, 1], jnp.arange(wide)[:, None] - line_row[None, :] + reach)
    depth_taps = depth_taps.transpose(1, 0, 2).reshape(tall, view_count * area)
    row_taps = row_taps.transpose(1, 0, 2).reshape(wide, view_count * area)
    sheet = (depth_taps[:, None, :] * row_taps[None, :, :]).astype(jnp.bfloat16)
    sheet = sheet.reshape(tall * wide, view_count * area)
    column = jnp.concatenate(
        [jnp.arange(cols), jnp.arange(-side, 0), jnp.arange(cols, cols + side)]
    )
    col_taps = taps_table(
        kernels[:, 2], column[:, None] - jnp.arange(cols)[None, :] + radius
    ).astype(jnp.bfloat16)

    own, tile_place, _ = lax.optimization_barrier((own, tile_place, sheet))

    def late_exchange():
        late_table = table(usual, lanes - usual)
        return exchange_by_permutes(pack(late_table[0], tiles)), late_table[1]

    def no_exchange():
        shape = (gy_count, lanes - usual)
        return jnp.zeros(shape + tiles.shape[1:], tiles.dtype), jnp.zeros(shape, jnp.int32)

    late, late_cell = lax.cond(
        most_slots(tile_place, positions) > usual, late_exchange, no_exchange
    )
    own = jnp.concatenate([shift(own, "gy", 1), own, shift(own, "gy", -1)], axis=1)
    own = jnp.concatenate([shift(own, "gz", 1), own, shift(own, "gz", -1)], axis=0)
    own = own.reshape(tall * wide, cols)
    groups = cols // side
    before = unpack_columns(shift(pack_columns(own[:, cols - side :], groups), "gx", 1), groups)
    after = unpack_columns(shift(pack_columns(own[:, :side], groups), "gx", -1), groups)
    field = jnp.concatenate([own, before, after], axis=1)
    swept = lax.dot_general(
        sheet, field, (((0,), (0,)), ((), ())), preferred_element_type=jnp.float32
    )
    swept = swept.astype(jnp.bfloat16).reshape(view_count, area, -1)
    blurred = jnp.einsum("vac,vck->vak", swept, col_taps, preferred_element_type=jnp.float32)
    joined = [
        ring_sum(join(c, ends, usual_table[1], late_cell, arrived, late, gz_count, chunk * positions))
        for c in range(chunks)
    ]
    joined = jnp.concatenate(joined).reshape(view_count, area, cols)

    ratio = (joined / (blurred + background_level)).astype(jnp.bfloat16)

    spread = jnp.einsum("vak,vck->vac", ratio, col_taps, preferred_element_type=jnp.float32)
    spread = spread.astype(jnp.bfloat16).reshape(view_count * area, -1)
    total = jnp.dot(sheet, spread, preferred_element_type=jnp.float32)
    leftward = pack_columns(total[:, cols : cols + side], groups).astype(jnp.bfloat16)
    rightward = pack_columns(total[:, cols + side :], groups).astype(jnp.bfloat16)
    from_right = unpack_columns(shift(leftward, "gx", -1), groups).astype(jnp.float32)
    from_left = unpack_columns(shift(rightward, "gx", 1), groups).astype(jnp.float32)
    edge = jnp.zeros((tall * wide, cols - 2 * side), jnp.float32)
    total = total[:, :cols] + jnp.concatenate([from_left, edge, from_right], axis=1)
    total = total.reshape(tall, wide, cols)
    upper = shift(total[:side].astype(jnp.bfloat16), "gz", -1)
    lower = shift(total[tall - side :].astype(jnp.bfloat16), "gz", 1)
    total = total[side : side + depth] + upper.astype(jnp.float32) + lower.astype(jnp.float32)
    upper = shift(total[:, :side], "gy", -1)
    lower = shift(total[:, wide - side :], "gy", 1)
    total = total[:, side : side + rows] + upper + lower
    return estimate * total / view_count


def solution(mesh):
    placed = (P(None, ("gz", "gy"), None, None, "gx"), P(), P(), P("gz", "gy", "gx"))
    return jax.shard_map(
        on_device, mesh=mesh, in_specs=placed, out_specs=P("gz", "gy", "gx"), check_vma=False
    )
```

```python
import functools

import jax
import jax.numpy as jnp
from jax import lax
from jax.experimental import pallas as pl
from jax.experimental.pallas import tpu as pltpu
from jax.sharding import PartitionSpec as P

background_level = 0.1
highest = lax.Precision.HIGHEST
capacity = 2
usual_slots = 56
smem = pl.BlockSpec(memory_space=pltpu.SMEM)
vmem = pl.BlockSpec(memory_space=pltpu.VMEM)


def neighbours(upward, downward, axis):
    devices = lax.axis_size(axis)
    even = lax.axis_index(axis) % 2 == 0
    first = jnp.where(even, upward, downward)
    second = jnp.where(even, downward, upward)
    bonds = [(i, i + 1) for i in range(devices - 1)]
    pairs = [[p for i, j in bonds[odd::2] for p in ((i, j), (j, i))] for odd in (0, 1)]
    return lax.ppermute(first, axis, pairs[0]), lax.ppermute(second, axis, pairs[1])


def from_sides(upward, downward, axis):
    even = lax.axis_index(axis) % 2 == 0
    first, second = neighbours(upward, downward, axis)
    return jnp.where(even, second, first), jnp.where(even, first, second)


def edges_kernel(value, last, first):
    rows, cols = last.shape
    groups = value.shape[0] // rows
    side = cols // groups
    group_of = lax.broadcasted_iota(jnp.int32, (rows, cols), 1) // side
    lasts = firsts = jnp.zeros((rows, cols), jnp.float32)
    for g in range(groups):
        block = value[g * rows : (g + 1) * rows].astype(jnp.float32)
        lasts = jnp.where(group_of == g, pltpu.roll(block, (g + 1) * side % cols, 1), lasts)
        firsts = jnp.where(group_of == g, pltpu.roll(block, g * side, 1), firsts)
    last[...] = lasts.astype(last.dtype)
    first[...] = firsts.astype(first.dtype)


def widen_kernel(value, before, after, wide):
    rows, cols = before.shape
    groups = value.shape[0] // rows
    side = cols // groups
    lane = lax.broadcasted_iota(jnp.int32, (rows, cols), 1)
    befores, afters = before[...].astype(jnp.float32), after[...].astype(jnp.float32)
    for g in range(groups):
        part = slice(g * rows, (g + 1) * rows)
        left = pltpu.roll(befores, (cols - g * side) % cols, 1)
        right = pltpu.roll(afters, (cols + side - g * side) % cols, 1)
        halo = jnp.where(lane < side, left, jnp.where(lane < 2 * side, right, 0.0))
        wide[part, :cols] = value[part]
        wide[part, cols:] = halo.astype(wide.dtype)


def with_columns(value, side):
    rows, cols = value.shape
    groups = cols // side
    packed = jax.ShapeDtypeStruct((rows // groups, cols), value.dtype)
    last, first = pl.pallas_call(
        edges_kernel,
        out_shape=[packed, packed],
        in_specs=[vmem],
        out_specs=[vmem, vmem],
        compiler_params=pltpu.CompilerParams(vmem_limit_bytes=32 << 20),
        name="edges",
    )(value)
    before, after = from_sides(last, first, "gx")
    return pl.pallas_call(
        widen_kernel,
        out_shape=jax.ShapeDtypeStruct((rows, 2 * cols), value.dtype),
        in_specs=[vmem] * 3,
        out_specs=vmem,
        compiler_params=pltpu.CompilerParams(vmem_limit_bytes=32 << 20),
        name="widen",
    )(value, before, after)


def taps_table(kernel_set, offset):
    taps = kernel_set.shape[-1]
    table = (offset[:, :, None] == jnp.arange(taps)[None, None, :]).astype(jnp.float32)
    return jnp.einsum("eim,vm->vei", table, kernel_set, precision=highest)


def slot_tables(tile_place, positions, chunks, usual):
    view_count = tile_place.shape[0]
    gz_count, gy_count = lax.axis_size("gz"), lax.axis_size("gy")
    my_gz, my_gy = lax.axis_index("gz"), lax.axis_index("gy")
    chunk = view_count // chunks
    placed = tile_place.reshape(view_count, gz_count, gy_count, -1)
    slot_count = placed.shape[-1]
    entries = view_count * slot_count
    group = lax.dynamic_index_in_dim(placed, my_gz, 1, keepdims=False)
    group = group.transpose(1, 0, 2).reshape(gy_count, entries)
    destination = group // positions
    dest_gy = destination % gy_count
    ahead = (destination // gy_count - my_gz) % gz_count
    view = jnp.arange(entries) // slot_count % chunk
    cell = (ahead * chunk + view) * positions + group % positions
    own_dest = lax.dynamic_index_in_dim(dest_gy, my_gy, 0, keepdims=True)
    sends = own_dest == jnp.arange(gy_count)[:, None]
    takes = dest_gy == my_gy
    number = jnp.broadcast_to(jnp.arange(entries)[None, :], takes.shape)
    chosen = jnp.stack([sends, takes])
    value = jnp.stack([number, cell])
    upto = (jnp.arange(entries)[:, None] <= jnp.arange(entries)[None, :]).astype(jnp.bfloat16)
    rank = jnp.dot(chosen.astype(jnp.bfloat16), upto, preferred_element_type=jnp.float32)
    rank = jnp.where(chosen, rank.astype(jnp.int32) - 1, -1)

    def table(first, lanes):
        hit = rank[..., None, :] == first + jnp.arange(lanes)[:, None]
        return jnp.sum(jnp.where(hit, value[..., None, :], 0), axis=-1).astype(jnp.int32)

    ends = [
        jnp.sum(takes[:, : c * chunk * slot_count], axis=-1).astype(jnp.int32)
        for c in range(chunks + 1)
    ]
    return table, jnp.stack(ends)


def most_slots(tile_place, positions):
    gy_count = lax.axis_size("gy")
    route_count = lax.axis_size(("gz", "gy"))
    dest_gy = (tile_place // positions) % gy_count
    dest_gy = dest_gy.reshape(tile_place.shape[0], route_count, 1, -1)
    return jnp.max(jnp.sum(dest_gy == jnp.arange(gy_count)[:, None], axis=(0, 3)))


def pack_kernel(source, tiles, outgoing):
    partners, lanes = outgoing.shape[:2]
    for partner in range(partners):
        for lane in range(lanes):
            outgoing[partner, lane] = tiles[source[partner, lane]]


def join_kernel(chunk, ends, cell, late_cell, arrived, late, *blocks_and_total):
    blocks, total = blocks_and_total[:-1], blocks_and_total[-1]
    partners, usual = arrived.shape[:2]
    step = 16

    def clear(index, carry):
        total[pl.ds(index * step, step)] = jnp.zeros((step,) + total.shape[1:], total.dtype)
        return carry

    lax.fori_loop(0, total.shape[0] // step, clear, 0)

    def add(cells, tiles, partner, lane):
        place = cells[partner, lane]
        total[place] = add_rounded(total[place], tiles[partner, lane])

    for partner in range(partners):
        first, last = ends[chunk, partner], ends[chunk + 1, partner]

        def add_usual(lane, carry):
            add(cell, arrived, partner, lane)
            return carry

        def add_late(lane, carry):
            add(late_cell, late, partner, lane - usual)
            return carry

        lax.fori_loop(jnp.minimum(first, usual), jnp.minimum(last, usual), add_usual, 0)
        lax.fori_loop(jnp.maximum(first, usual), jnp.maximum(last, usual), add_late, 0)
    start = 0
    for block in blocks:
        block[...] = total[start : start + block.shape[0]]
        start += block.shape[0]


def pack(source, tiles):
    return pl.pallas_call(
        pack_kernel,
        out_shape=jax.ShapeDtypeStruct(source.shape + tiles.shape[1:], tiles.dtype),
        in_specs=[smem, vmem],
        out_specs=vmem,
        compiler_params=pltpu.CompilerParams(vmem_limit_bytes=32 << 20),
        name="pack",
    )(source, tiles)


def join(chunk, ends, cell, late_cell, arrived, late, devices, cells):
    tile = arrived.shape[2:]
    half = devices // 2
    sizes = [cells] * half + [cells // 2] * 2 + [cells] * (half - 1)
    return pl.pallas_call(
        functools.partial(join_kernel, chunk),
        out_shape=[jax.ShapeDtypeStruct((size,) + tile, arrived.dtype) for size in sizes],
        in_specs=[smem, smem, smem, vmem, vmem],
        out_specs=[vmem] * len(sizes),
        scratch_shapes=[pltpu.VMEM((devices * cells,) + tile, arrived.dtype)],
        compiler_params=pltpu.CompilerParams(vmem_limit_bytes=32 << 20),
        name="join",
    )(ends, cell, late_cell, arrived, late)


def exchange(value):
    return lax.all_to_all(value, "gy", split_axis=0, concat_axis=0, tiled=True)


def exchange_by_permutes(value):
    devices, me = lax.axis_size("gy"), lax.axis_index("gy")
    result = value
    for step in range(1, devices):
        part = lax.dynamic_index_in_dim(value, (me + step) % devices, 0)
        part = lax.ppermute(part, "gy", [(i, (i + step) % devices) for i in range(devices)])
        result = lax.dynamic_update_index_in_dim(result, part, (me - step) % devices, 0)
    return result


def add_rounded(left, right):
    return (left.astype(jnp.float32) + right.astype(jnp.float32)).astype(left.dtype)


def ring_sum(blocks):
    devices = len(blocks) - 1
    half = devices // 2
    up = [(i, (i + 1) % devices) for i in range(devices)]
    down = [(j, i) for i, j in up]
    middle = blocks[half].shape[0]
    from_below = lax.ppermute(blocks[half], "gz", up)
    from_above = lax.ppermute(blocks[half + 1], "gz", down)
    for ahead in range(half - 1, 0, -1):
        upward, downward = blocks[ahead], blocks[devices - ahead + 1]
        if ahead == half - 1:
            upward = jnp.concatenate([add_rounded(upward[:middle], from_below), upward[middle:]])
            downward = jnp.concatenate(
                [downward[:middle], add_rounded(downward[middle:], from_above)]
            )
        else:
            upward = add_rounded(upward, from_below)
            downward = add_rounded(downward, from_above)
        from_below = lax.ppermute(upward, "gz", up)
        from_above = lax.ppermute(downward, "gz", down)
    return (
        blocks[0].astype(jnp.float32)
        + from_below.astype(jnp.float32)
        + from_above.astype(jnp.float32)
    )


def on_device(recorded, tile_place, psf, estimate):
    view_count = recorded.shape[0]
    tile_depth, tile_rows = recorded.shape[2:4]
    depth, rows, cols = estimate.shape
    per_row = rows // tile_rows
    positions = depth // tile_depth * per_row
    area = depth * rows
    radius = (psf.shape[2] - 1) // 2
    side = 16
    tall, wide = depth + 2 * side, rows + 2 * side
    chunks = 2
    chunk = view_count // chunks
    gz_count, gy_count = lax.axis_size("gz"), lax.axis_size("gy")
    tiles = recorded.reshape(-1, tile_depth * tile_rows, cols)
    lanes = gz_count * capacity * view_count
    usual = min(usual_slots, lanes)
    table, ends = slot_tables(tile_place, positions, chunks, usual)
    usual_table = table(0, usual)
    outgoing, psf = lax.optimization_barrier((pack(usual_table[0], tiles), psf))
    arrived = exchange(outgoing)
    own = estimate.astype(jnp.bfloat16)

    kernels = psf / jnp.sum(psf, axis=-1, keepdims=True)
    line = jnp.arange(area)
    place, inside = line // (tile_depth * tile_rows), line % (tile_depth * tile_rows)
    line_depth = place // per_row * tile_depth + inside // tile_rows
    line_row = place % per_row * tile_rows + inside % tile_rows
    reach = radius - side
    depth_taps = taps_table(kernels[:, 0], jnp.arange(tall)[:, None] - line_depth[None, :] + reach)
    row_taps = taps_table(kernels[:, 1], jnp.arange(wide)[:, None] - line_row[None, :] + reach)
    sheets = []
    for v in range(0, view_count, chunk):
        down = depth_taps[v : v + chunk].transpose(1, 0, 2).reshape(tall, 1, chunk * area)
        across = row_taps[v : v + chunk].transpose(1, 0, 2).reshape(1, wide, chunk * area)
        sheet = (down * across).astype(jnp.bfloat16)
        sheets.append(sheet.reshape(tall * wide, chunk * area))
    column = jnp.concatenate(
        [jnp.arange(cols), jnp.arange(-side, 0), jnp.arange(cols, cols + side)]
        + [jnp.full(cols - 2 * side, -cols)]
    )
    offset = column[:, None] - jnp.arange(cols)[None, :]
    col_taps = taps_table(kernels[:, 2], radius + offset).astype(jnp.bfloat16)
    col_taps_back = taps_table(kernels[:, 2], radius - offset).astype(jnp.bfloat16)

    own, tile_place, _ = lax.optimization_barrier((own, tile_place, sheets))

    def late_exchange():
        late_table = table(usual, lanes - usual)
        return exchange_by_permutes(pack(late_table[0], tiles)), late_table[1]

    def no_exchange():
        shape = (gy_count, lanes - usual)
        return jnp.zeros(shape + tiles.shape[1:], tiles.dtype), jnp.zeros(shape, jnp.int32)

    overflows = most_slots(tile_place, positions) > usual
    above, below = from_sides(own, own, "gy")
    own = jnp.concatenate([above, own, below], axis=1)
    above, below = from_sides(own, own, "gz")
    own = jnp.concatenate([above, own, below], axis=0)
    own = own.reshape(tall * wide, cols)
    own, arrived, overflows = lax.optimization_barrier((own, arrived, overflows))
    late, late_cell = lax.cond(overflows, late_exchange, no_exchange)
    field = with_columns(own, side)
    total = jnp.zeros((tall * wide, cols), jnp.float32)
    joined = [
        ring_sum(join(c, ends, usual_table[1], late_cell, arrived, late, gz_count, chunk * positions))
        for c in range(chunks)
    ]
    for c in range(chunks):
        views = slice(c * chunk, (c + 1) * chunk)
        swept = lax.dot_general(
            sheets[c], field, (((0,), (0,)), ((), ())), preferred_element_type=jnp.float32
        )
        swept = swept.astype(jnp.bfloat16).reshape(chunk, area, -1)
        blurred = jnp.einsum(
            "vac,vck->vak", swept, col_taps[views], preferred_element_type=jnp.float32
        )
        ratio = joined[c].reshape(chunk, area, cols) / (blurred + background_level)
        ratio = ratio.astype(jnp.bfloat16).reshape(chunk * area, cols)
        ratio = with_columns(ratio, side).reshape(chunk, area, -1)
        spread = jnp.einsum(
            "vac,vck->vak", ratio, col_taps_back[views], preferred_element_type=jnp.float32
        )
        spread = spread.astype(jnp.bfloat16).reshape(chunk * area, cols)
        total = total + jnp.dot(sheets[c], spread, preferred_element_type=jnp.float32)
    total = total.reshape(tall, wide, cols)
    first, second = neighbours(
        total[side + depth :].astype(jnp.float16), total[:side].astype(jnp.float16), "gz"
    )
    total = total[side : side + depth] + first.astype(jnp.float32) + second.astype(jnp.float32)
    first, second = neighbours(
        total[:, side + rows :].astype(jnp.float16), total[:, :side].astype(jnp.float16), "gy"
    )
    result = total[:, side : side + rows] + first.astype(jnp.float32) + second.astype(jnp.float32)
    return estimate * result / view_count


def solution(mesh):
    placed = (P(None, ("gz", "gy"), None, None, "gx"), P(), P(), P("gz", "gy", "gx"))
    return jax.shard_map(
        on_device, mesh=mesh, in_specs=placed, out_specs=P("gz", "gy", "gx"), check_vma=False
    )
```

```python
import functools

import jax
import jax.numpy as jnp
from jax import lax
from jax.experimental import pallas as pl
from jax.experimental.pallas import tpu as pltpu
from jax.sharding import PartitionSpec as P

background_level = 0.1
highest = lax.Precision.HIGHEST
capacity = 2
usual_slots = 56
smem = pl.BlockSpec(memory_space=pltpu.SMEM)
vmem = pl.BlockSpec(memory_space=pltpu.VMEM)


def neighbours(upward, downward, axis):
    devices = lax.axis_size(axis)
    even = lax.axis_index(axis) % 2 == 0
    first = jnp.where(even, upward, downward)
    second = jnp.where(even, downward, upward)
    bonds = [(i, i + 1) for i in range(devices - 1)]
    pairs = [[p for i, j in bonds[odd::2] for p in ((i, j), (j, i))] for odd in (0, 1)]
    return lax.ppermute(first, axis, pairs[0]), lax.ppermute(second, axis, pairs[1])


def from_sides(upward, downward, axis):
    even = lax.axis_index(axis) % 2 == 0
    first, second = neighbours(upward, downward, axis)
    return jnp.where(even, second, first), jnp.where(even, first, second)


def edges_kernel(value, last, first):
    rows, cols = last.shape
    groups = value.shape[0] // rows
    side = cols // groups
    group_of = lax.broadcasted_iota(jnp.int32, (rows, cols), 1) // side
    lasts = firsts = jnp.zeros((rows, cols), jnp.float32)
    for g in range(groups):
        block = value[g * rows : (g + 1) * rows].astype(jnp.float32)
        lasts = jnp.where(group_of == g, pltpu.roll(block, (g + 1) * side % cols, 1), lasts)
        firsts = jnp.where(group_of == g, pltpu.roll(block, g * side, 1), firsts)
    last[...] = lasts.astype(last.dtype)
    first[...] = firsts.astype(first.dtype)


def widen_kernel(value, before, after, wide):
    rows, cols = before.shape
    groups = value.shape[0] // rows
    side = cols // groups
    lane = lax.broadcasted_iota(jnp.int32, (rows, cols), 1)
    befores, afters = before[...].astype(jnp.float32), after[...].astype(jnp.float32)
    for g in range(groups):
        part = slice(g * rows, (g + 1) * rows)
        left = pltpu.roll(befores, (cols - g * side) % cols, 1)
        right = pltpu.roll(afters, (cols + side - g * side) % cols, 1)
        halo = jnp.where(lane < side, left, jnp.where(lane < 2 * side, right, 0.0))
        wide[part, :cols] = value[part]
        wide[part, cols:] = halo.astype(wide.dtype)


def with_columns(value, side):
    rows, cols = value.shape
    groups = cols // side
    packed = jax.ShapeDtypeStruct((rows // groups, cols), value.dtype)
    last, first = pl.pallas_call(
        edges_kernel,
        out_shape=[packed, packed],
        in_specs=[vmem],
        out_specs=[vmem, vmem],
        compiler_params=pltpu.CompilerParams(vmem_limit_bytes=32 << 20),
        name="edges",
    )(value)
    before, after = from_sides(last, first, "gx")
    return pl.pallas_call(
        widen_kernel,
        out_shape=jax.ShapeDtypeStruct((rows, 2 * cols), value.dtype),
        in_specs=[vmem] * 3,
        out_specs=vmem,
        compiler_params=pltpu.CompilerParams(vmem_limit_bytes=32 << 20),
        name="widen",
    )(value, before, after)


def taps_table(kernel_set, offset):
    taps = kernel_set.shape[-1]
    table = (offset[:, :, None] == jnp.arange(taps)[None, None, :]).astype(jnp.float32)
    return jnp.einsum("eim,vm->vei", table, kernel_set, precision=highest)


def slot_tables(tile_place, positions, chunks, usual):
    view_count = tile_place.shape[0]
    gz_count, gy_count = lax.axis_size("gz"), lax.axis_size("gy")
    my_gz, my_gy = lax.axis_index("gz"), lax.axis_index("gy")
    chunk = view_count // chunks
    placed = tile_place.reshape(view_count, gz_count, gy_count, -1)
    slot_count = placed.shape[-1]
    entries = view_count * slot_count
    group = lax.dynamic_index_in_dim(placed, my_gz, 1, keepdims=False)
    group = group.transpose(1, 0, 2).reshape(gy_count, entries)
    destination = group // positions
    dest_gy = destination % gy_count
    ahead = (destination // gy_count - my_gz) % gz_count
    view = jnp.arange(entries) // slot_count % chunk
    cell = (ahead * chunk + view) * positions + group % positions
    own_dest = lax.dynamic_index_in_dim(dest_gy, my_gy, 0, keepdims=True)
    sends = own_dest == jnp.arange(gy_count)[:, None]
    takes = dest_gy == my_gy
    number = jnp.broadcast_to(jnp.arange(entries)[None, :], takes.shape)
    chosen = jnp.stack([sends, takes])
    value = jnp.stack([number, cell])
    upto = (jnp.arange(entries)[:, None] <= jnp.arange(entries)[None, :]).astype(jnp.bfloat16)
    rank = jnp.dot(chosen.astype(jnp.bfloat16), upto, preferred_element_type=jnp.float32)
    rank = jnp.where(chosen, rank.astype(jnp.int32) - 1, -1)

    def table(first, lanes):
        hit = rank[..., None, :] == first + jnp.arange(lanes)[:, None]
        return jnp.sum(jnp.where(hit, value[..., None, :], 0), axis=-1).astype(jnp.int32)

    ends = [
        jnp.sum(takes[:, : c * chunk * slot_count], axis=-1).astype(jnp.int32)
        for c in range(chunks + 1)
    ]
    return table, jnp.stack(ends)


def most_slots(tile_place, positions):
    gy_count = lax.axis_size("gy")
    route_count = lax.axis_size(("gz", "gy"))
    dest_gy = (tile_place // positions) % gy_count
    dest_gy = dest_gy.reshape(tile_place.shape[0], route_count, 1, -1)
    return jnp.max(jnp.sum(dest_gy == jnp.arange(gy_count)[:, None], axis=(0, 3)))


def pack_kernel(source, tiles, outgoing):
    partners, lanes = outgoing.shape[:2]
    for partner in range(partners):
        for lane in range(lanes):
            outgoing[partner, lane] = tiles[source[partner, lane]]


def join_kernel(chunk, ends, cell, late_cell, arrived, late, *blocks_and_total):
    blocks, total = blocks_and_total[:-1], blocks_and_total[-1]
    partners, usual = arrived.shape[:2]
    step = 16

    def clear(index, carry):
        total[pl.ds(index * step, step)] = jnp.zeros((step,) + total.shape[1:], total.dtype)
        return carry

    lax.fori_loop(0, total.shape[0] // step, clear, 0)

    def add(cells, tiles, partner, lane):
        place = cells[partner, lane]
        total[place] = add_rounded(total[place], tiles[partner, lane])

    for partner in range(partners):
        first, last = ends[chunk, partner], ends[chunk + 1, partner]

        def add_usual(lane, carry):
            add(cell, arrived, partner, lane)
            return carry

        def add_late(lane, carry):
            add(late_cell, late, partner, lane - usual)
            return carry

        lax.fori_loop(jnp.minimum(first, usual), jnp.minimum(last, usual), add_usual, 0)
        lax.fori_loop(jnp.maximum(first, usual), jnp.maximum(last, usual), add_late, 0)
    start = 0
    for block in blocks:
        block[...] = total[start : start + block.shape[0]]
        start += block.shape[0]


def pack(source, tiles):
    return pl.pallas_call(
        pack_kernel,
        out_shape=jax.ShapeDtypeStruct(source.shape + tiles.shape[1:], tiles.dtype),
        in_specs=[smem, vmem],
        out_specs=vmem,
        compiler_params=pltpu.CompilerParams(vmem_limit_bytes=32 << 20),
        name="pack",
    )(source, tiles)


def join(chunk, ends, cell, late_cell, arrived, late, devices, cells):
    tile = arrived.shape[2:]
    half = devices // 2
    sizes = [cells] * half + [cells // 2] * 2 + [cells] * (half - 1)
    return pl.pallas_call(
        functools.partial(join_kernel, chunk),
        out_shape=[jax.ShapeDtypeStruct((size,) + tile, arrived.dtype) for size in sizes],
        in_specs=[smem, smem, smem, vmem, vmem],
        out_specs=[vmem] * len(sizes),
        scratch_shapes=[pltpu.VMEM((devices * cells,) + tile, arrived.dtype)],
        compiler_params=pltpu.CompilerParams(vmem_limit_bytes=32 << 20),
        name="join",
    )(ends, cell, late_cell, arrived, late)


def unwritten(shape, dtype):
    return pl.pallas_call(
        lambda out: None,
        out_shape=jax.ShapeDtypeStruct(shape, dtype),
        out_specs=pl.BlockSpec(memory_space=pl.ANY),
        name="unwritten",
    )()


def exchange(value):
    return lax.all_to_all(value, "gy", split_axis=0, concat_axis=0, tiled=True)


def exchange_by_permutes(value):
    devices, me = lax.axis_size("gy"), lax.axis_index("gy")
    result = value
    for step in range(1, devices):
        part = lax.dynamic_index_in_dim(value, (me + step) % devices, 0)
        part = lax.ppermute(part, "gy", [(i, (i + step) % devices) for i in range(devices)])
        result = lax.dynamic_update_index_in_dim(result, part, (me - step) % devices, 0)
    return result


def add_rounded(left, right):
    return (left.astype(jnp.float32) + right.astype(jnp.float32)).astype(left.dtype)


def ring_sum(blocks):
    devices = len(blocks) - 1
    half = devices // 2
    up = [(i, (i + 1) % devices) for i in range(devices)]
    down = [(j, i) for i, j in up]
    middle = blocks[half].shape[0]
    from_below = lax.ppermute(blocks[half], "gz", up)
    from_above = lax.ppermute(blocks[half + 1], "gz", down)
    for ahead in range(half - 1, 0, -1):
        upward, downward = blocks[ahead], blocks[devices - ahead + 1]
        if ahead == half - 1:
            upward = jnp.concatenate([add_rounded(upward[:middle], from_below), upward[middle:]])
            downward = jnp.concatenate(
                [downward[:middle], add_rounded(downward[middle:], from_above)]
            )
        else:
            upward = add_rounded(upward, from_below)
            downward = add_rounded(downward, from_above)
        from_below = lax.ppermute(upward, "gz", up)
        from_above = lax.ppermute(downward, "gz", down)
    return (
        blocks[0].astype(jnp.float32)
        + from_below.astype(jnp.float32)
        + from_above.astype(jnp.float32)
    )


def on_device(recorded, tile_place, psf, estimate):
    view_count = recorded.shape[0]
    tile_depth, tile_rows = recorded.shape[2:4]
    depth, rows, cols = estimate.shape
    per_row = rows // tile_rows
    positions = depth // tile_depth * per_row
    area = depth * rows
    radius = (psf.shape[2] - 1) // 2
    side = 16
    tall, wide = depth + 2 * side, rows + 2 * side
    chunks = 2
    chunk = view_count // chunks
    gz_count, gy_count = lax.axis_size("gz"), lax.axis_size("gy")
    tiles = recorded.reshape(-1, tile_depth * tile_rows, cols)
    lanes = gz_count * capacity * view_count
    usual = min(usual_slots, lanes)
    table, ends = slot_tables(tile_place, positions, chunks, usual)
    usual_table = table(0, usual)

    def late_exchange():
        late_table = table(usual, lanes - usual)
        return exchange_by_permutes(pack(late_table[0], tiles)), late_table[1]

    def no_exchange():
        shape = (gy_count, lanes - usual)
        return unwritten(shape + tiles.shape[1:], tiles.dtype), jnp.zeros(shape, jnp.int32)

    late, late_cell = lax.cond(
        most_slots(tile_place, positions) > usual, late_exchange, no_exchange
    )
    usual_table, late_cell = lax.optimization_barrier((usual_table, late_cell))
    outgoing, psf = lax.optimization_barrier((pack(usual_table[0], tiles), psf))
    arrived = exchange(outgoing)
    own = estimate.astype(jnp.bfloat16)

    kernels = psf / jnp.sum(psf, axis=-1, keepdims=True)
    line = jnp.arange(area)
    place, inside = line // (tile_depth * tile_rows), line % (tile_depth * tile_rows)
    line_depth = place // per_row * tile_depth + inside // tile_rows
    line_row = place % per_row * tile_rows + inside % tile_rows
    reach = radius - side
    depth_taps = taps_table(kernels[:, 0], jnp.arange(tall)[:, None] - line_depth[None, :] + reach)
    row_taps = taps_table(kernels[:, 1], jnp.arange(wide)[:, None] - line_row[None, :] + reach)
    sheets = []
    for v in range(0, view_count, chunk):
        down = depth_taps[v : v + chunk].transpose(1, 0, 2).reshape(tall, 1, chunk * area)
        across = row_taps[v : v + chunk].transpose(1, 0, 2).reshape(1, wide, chunk * area)
        sheet = (down * across).astype(jnp.bfloat16)
        sheets.append(sheet.reshape(tall * wide, chunk * area))
    own, _ = lax.optimization_barrier((own, sheets))
    above, below = from_sides(own, own, "gy")
    own = jnp.concatenate([above, own, below], axis=1)
    own, arrived, column_kernels = lax.optimization_barrier((own, arrived, kernels[:, 2]))
    above, below = from_sides(own, own, "gz")
    own = jnp.concatenate([above, own, below], axis=0)
    own = own.reshape(tall * wide, cols)
    column = jnp.concatenate(
        [jnp.arange(cols), jnp.arange(-side, 0), jnp.arange(cols, cols + side)]
        + [jnp.full(cols - 2 * side, -cols)]
    )
    offset = column[:, None] - jnp.arange(cols)[None, :]
    col_taps = taps_table(column_kernels, radius + offset).astype(jnp.bfloat16)
    col_taps_back = taps_table(column_kernels, radius - offset).astype(jnp.bfloat16)
    field = with_columns(own, side)
    total = jnp.zeros((tall * wide, cols), jnp.float32)
    joined = [
        ring_sum(join(c, ends, usual_table[1], late_cell, arrived, late, gz_count, chunk * positions))
        for c in range(chunks)
    ]
    for c in range(chunks):
        views = slice(c * chunk, (c + 1) * chunk)
        swept = lax.dot_general(
            sheets[c], field, (((0,), (0,)), ((), ())), preferred_element_type=jnp.float32
        )
        swept = swept.astype(jnp.bfloat16).reshape(chunk, area, -1)
        blurred = jnp.einsum(
            "vac,vck->vak", swept, col_taps[views], preferred_element_type=jnp.float32
        )
        ratio = joined[c].reshape(chunk, area, cols) / (blurred + background_level)
        ratio = ratio.astype(jnp.bfloat16).reshape(chunk * area, cols)
        ratio = with_columns(ratio, side).reshape(chunk, area, -1)
        spread = jnp.einsum(
            "vac,vck->vak", ratio, col_taps_back[views], preferred_element_type=jnp.float32
        )
        spread = spread.astype(jnp.bfloat16).reshape(chunk * area, cols)
        total = total + jnp.dot(sheets[c], spread, preferred_element_type=jnp.float32)
    total = total.reshape(tall, wide, cols)
    first, second = neighbours(
        total[side + depth :].astype(jnp.float16), total[:side].astype(jnp.float16), "gz"
    )
    total = total[side : side + depth] + first.astype(jnp.float32) + second.astype(jnp.float32)
    first, second = neighbours(
        total[:, side + rows :].astype(jnp.float16), total[:, :side].astype(jnp.float16), "gy"
    )
    result = total[:, side : side + rows] + first.astype(jnp.float32) + second.astype(jnp.float32)
    return estimate * result / view_count


def solution(mesh):
    placed = (P(None, ("gz", "gy"), None, None, "gx"), P(), P(), P("gz", "gy", "gx"))
    return jax.shard_map(
        on_device, mesh=mesh, in_specs=placed, out_specs=P("gz", "gy", "gx"), check_vma=False
    )
```

```python
import functools

import jax
import jax.numpy as jnp
from jax import lax
from jax.experimental import pallas as pl
from jax.experimental.pallas import tpu as pltpu
from jax.sharding import PartitionSpec as P

background_level = 0.1
highest = lax.Precision.HIGHEST
capacity = 2
usual_slots = 56
smem = pl.BlockSpec(memory_space=pltpu.SMEM)
vmem = pl.BlockSpec(memory_space=pltpu.VMEM)


def neighbours(upward, downward, axis):
    devices = lax.axis_size(axis)
    even = lax.axis_index(axis) % 2 == 0
    first = jnp.where(even, upward, downward)
    second = jnp.where(even, downward, upward)
    bonds = [(i, i + 1) for i in range(devices - 1)]
    pairs = [[p for i, j in bonds[odd::2] for p in ((i, j), (j, i))] for odd in (0, 1)]
    return lax.ppermute(first, axis, pairs[0]), lax.ppermute(second, axis, pairs[1])


def from_sides(upward, downward, axis):
    even = lax.axis_index(axis) % 2 == 0
    first, second = neighbours(upward, downward, axis)
    return jnp.where(even, second, first), jnp.where(even, first, second)


def edges_kernel(value, last, first):
    rows, cols = last.shape
    groups = value.shape[0] // rows
    side = cols // groups
    group_of = lax.broadcasted_iota(jnp.int32, (rows, cols), 1) // side
    lasts = firsts = jnp.zeros((rows, cols), jnp.float32)
    for g in range(groups):
        block = value[g * rows : (g + 1) * rows].astype(jnp.float32)
        lasts = jnp.where(group_of == g, pltpu.roll(block, (g + 1) * side % cols, 1), lasts)
        firsts = jnp.where(group_of == g, pltpu.roll(block, g * side, 1), firsts)
    last[...] = lasts.astype(last.dtype)
    first[...] = firsts.astype(first.dtype)


def widen_kernel(value, before, after, wide):
    rows, cols = before.shape
    groups = value.shape[0] // rows
    side = cols // groups
    lane = lax.broadcasted_iota(jnp.int32, (rows, cols), 1)
    befores, afters = before[...].astype(jnp.float32), after[...].astype(jnp.float32)
    for g in range(groups):
        part = slice(g * rows, (g + 1) * rows)
        left = pltpu.roll(befores, (cols - g * side) % cols, 1)
        right = pltpu.roll(afters, (cols + side - g * side) % cols, 1)
        halo = jnp.where(lane < side, left, jnp.where(lane < 2 * side, right, 0.0))
        wide[part, :cols] = value[part]
        wide[part, cols:] = halo.astype(wide.dtype)


def with_columns(value, side):
    rows, cols = value.shape
    groups = cols // side
    packed = jax.ShapeDtypeStruct((rows // groups, cols), value.dtype)
    last, first = pl.pallas_call(
        edges_kernel,
        out_shape=[packed, packed],
        in_specs=[vmem],
        out_specs=[vmem, vmem],
        compiler_params=pltpu.CompilerParams(vmem_limit_bytes=32 << 20),
        name="edges",
    )(value)
    before, after = from_sides(last, first, "gx")
    return pl.pallas_call(
        widen_kernel,
        out_shape=jax.ShapeDtypeStruct((rows, 2 * cols), value.dtype),
        in_specs=[vmem] * 3,
        out_specs=vmem,
        compiler_params=pltpu.CompilerParams(vmem_limit_bytes=32 << 20),
        name="widen",
    )(value, before, after)


def taps_table(kernel_set, offset):
    taps = kernel_set.shape[-1]
    table = (offset[:, :, None] == jnp.arange(taps)[None, None, :]).astype(jnp.float32)
    return jnp.einsum("eim,vm->vei", table, kernel_set, precision=highest)


def slot_tables(tile_place, positions, chunks, usual):
    view_count = tile_place.shape[0]
    gz_count, gy_count = lax.axis_size("gz"), lax.axis_size("gy")
    my_gz, my_gy = lax.axis_index("gz"), lax.axis_index("gy")
    chunk = view_count // chunks
    placed = tile_place.reshape(view_count, gz_count, gy_count, -1)
    slot_count = placed.shape[-1]
    entries = view_count * slot_count
    group = lax.dynamic_index_in_dim(placed, my_gz, 1, keepdims=False)
    group = group.transpose(1, 0, 2).reshape(gy_count, entries)
    destination = group // positions
    dest_gy = destination % gy_count
    ahead = (destination // gy_count - my_gz) % gz_count
    view = jnp.arange(entries) // slot_count % chunk
    cell = (ahead * chunk + view) * positions + group % positions
    own_dest = lax.dynamic_index_in_dim(dest_gy, my_gy, 0, keepdims=True)
    sends = own_dest == jnp.arange(gy_count)[:, None]
    takes = dest_gy == my_gy
    number = jnp.broadcast_to(jnp.arange(entries)[None, :], takes.shape)
    chosen = jnp.stack([sends, takes])
    value = jnp.stack([number, cell])
    upto = (jnp.arange(entries)[:, None] <= jnp.arange(entries)[None, :]).astype(jnp.bfloat16)
    rank = jnp.dot(chosen.astype(jnp.bfloat16), upto, preferred_element_type=jnp.float32)
    rank = jnp.where(chosen, rank.astype(jnp.int32) - 1, -1)

    def table(first, lanes):
        hit = rank[..., None, :] == first + jnp.arange(lanes)[:, None]
        return jnp.sum(jnp.where(hit, value[..., None, :], 0), axis=-1).astype(jnp.int32)

    ends = [
        jnp.sum(takes[:, : c * chunk * slot_count], axis=-1).astype(jnp.int32)
        for c in range(chunks + 1)
    ]
    return table, jnp.stack(ends)


def most_slots(tile_place, positions):
    gy_count = lax.axis_size("gy")
    route_count = lax.axis_size(("gz", "gy"))
    dest_gy = (tile_place // positions) % gy_count
    dest_gy = dest_gy.reshape(tile_place.shape[0], route_count, 1, -1)
    return jnp.max(jnp.sum(dest_gy == jnp.arange(gy_count)[:, None], axis=(0, 3)))


def pack_kernel(source, tiles, outgoing):
    partners, lanes = outgoing.shape[:2]

    def one(partner, carry):
        for lane in range(lanes):
            outgoing[partner, lane] = tiles[source[partner, lane]]
        return carry

    lax.fori_loop(0, partners, one, 0)


def join_kernel(chunk, ends, cell, late_cell, arrived, late, *blocks_and_total):
    blocks, total = blocks_and_total[:-1], blocks_and_total[-1]
    partners, usual = arrived.shape[:2]
    step = 16

    def clear(index, carry):
        total[pl.ds(index * step, step)] = jnp.zeros((step,) + total.shape[1:], total.dtype)
        return carry

    lax.fori_loop(0, total.shape[0] // step, clear, 0)

    def add(cells, tiles, partner, lane):
        place = cells[partner, lane]
        total[place] = add_rounded(total[place], tiles[partner, lane])

    for partner in range(partners):
        first, last = ends[chunk, partner], ends[chunk + 1, partner]

        def add_usual(lane, carry):
            add(cell, arrived, partner, lane)
            return carry

        def add_late(lane, carry):
            add(late_cell, late, partner, lane - usual)
            return carry

        lax.fori_loop(jnp.minimum(first, usual), jnp.minimum(last, usual), add_usual, 0)
        lax.fori_loop(jnp.maximum(first, usual), jnp.maximum(last, usual), add_late, 0)
    start = 0
    for block in blocks:
        block[...] = total[start : start + block.shape[0]]
        start += block.shape[0]


def pack(source, tiles):
    return pl.pallas_call(
        pack_kernel,
        out_shape=jax.ShapeDtypeStruct(source.shape + tiles.shape[1:], tiles.dtype),
        in_specs=[smem, vmem],
        out_specs=vmem,
        compiler_params=pltpu.CompilerParams(vmem_limit_bytes=32 << 20),
        name="pack",
    )(source, tiles)


def join(chunk, ends, cell, late_cell, arrived, late, devices, cells):
    tile = arrived.shape[2:]
    half = devices // 2
    sizes = [cells] * half + [cells // 2] * 2 + [cells] * (half - 1)
    return pl.pallas_call(
        functools.partial(join_kernel, chunk),
        out_shape=[jax.ShapeDtypeStruct((size,) + tile, arrived.dtype) for size in sizes],
        in_specs=[smem, smem, smem, vmem, vmem],
        out_specs=[vmem] * len(sizes),
        scratch_shapes=[pltpu.VMEM((devices * cells,) + tile, arrived.dtype)],
        compiler_params=pltpu.CompilerParams(vmem_limit_bytes=32 << 20),
        name="join",
    )(ends, cell, late_cell, arrived, late)


def unwritten(shape, dtype):
    return pl.pallas_call(
        lambda out: None,
        out_shape=jax.ShapeDtypeStruct(shape, dtype),
        out_specs=pl.BlockSpec(memory_space=pl.ANY),
        name="unwritten",
    )()


def exchange(value):
    return lax.all_to_all(value, "gy", split_axis=0, concat_axis=0, tiled=True)


def add_rounded(left, right):
    return (left.astype(jnp.float32) + right.astype(jnp.float32)).astype(left.dtype)


def ring_step(upward, downward):
    devices = lax.axis_size("gz")
    up = [(i, (i + 1) % devices) for i in range(devices)]
    down = [(j, i) for i, j in up]
    return lax.ppermute(upward, "gz", up), lax.ppermute(downward, "gz", down)


def ring_sum(blocks, from_below, from_above):
    devices = len(blocks) - 1
    half = devices // 2
    middle = blocks[half].shape[0]
    for ahead in range(half - 1, 0, -1):
        upward, downward = blocks[ahead], blocks[devices - ahead + 1]
        if ahead == half - 1:
            upward = jnp.concatenate([add_rounded(upward[:middle], from_below), upward[middle:]])
            downward = jnp.concatenate(
                [downward[:middle], add_rounded(downward[middle:], from_above)]
            )
        else:
            upward = add_rounded(upward, from_below)
            downward = add_rounded(downward, from_above)
        from_below, from_above = ring_step(upward, downward)
    return (
        blocks[0].astype(jnp.float32)
        + from_below.astype(jnp.float32)
        + from_above.astype(jnp.float32)
    )


def on_device(recorded, tile_place, psf, estimate):
    view_count = recorded.shape[0]
    tile_depth, tile_rows = recorded.shape[2:4]
    depth, rows, cols = estimate.shape
    per_row = rows // tile_rows
    positions = depth // tile_depth * per_row
    area = depth * rows
    radius = (psf.shape[2] - 1) // 2
    side = 16
    tall, wide = depth + 2 * side, rows + 2 * side
    chunks = 2
    chunk = view_count // chunks
    gz_count, gy_count = lax.axis_size("gz"), lax.axis_size("gy")
    tiles = recorded.reshape(-1, tile_depth * tile_rows, cols)
    lanes = gz_count * capacity * view_count
    usual = min(usual_slots, lanes)
    table, ends = slot_tables(tile_place, positions, chunks, usual)
    usual_table = table(0, usual)

    def late_exchange():
        late_table = table(usual, lanes - usual)
        return exchange(pack(late_table[0], tiles)), late_table[1]

    def no_exchange():
        shape = (gy_count, lanes - usual)
        return unwritten(shape + tiles.shape[1:], tiles.dtype), jnp.zeros(shape, jnp.int32)

    late, late_cell = lax.cond(
        most_slots(tile_place, positions) > usual, late_exchange, no_exchange
    )
    usual_table, late_cell = lax.optimization_barrier((usual_table, late_cell))
    outgoing, psf = lax.optimization_barrier((pack(usual_table[0], tiles), psf))
    arrived = exchange(outgoing)
    own = estimate.astype(jnp.bfloat16)

    kernels = psf / jnp.sum(psf, axis=-1, keepdims=True)
    line = jnp.arange(area)
    place, inside = line // (tile_depth * tile_rows), line % (tile_depth * tile_rows)
    line_depth = place // per_row * tile_depth + inside // tile_rows
    line_row = place % per_row * tile_rows + inside % tile_rows
    reach = radius - side
    depth_taps = taps_table(kernels[:, 0], jnp.arange(tall)[:, None] - line_depth[None, :] + reach)
    row_taps = taps_table(kernels[:, 1], jnp.arange(wide)[:, None] - line_row[None, :] + reach)
    sheets = []
    for v in range(0, view_count, chunk):
        down = depth_taps[v : v + chunk].transpose(1, 0, 2).reshape(tall, 1, chunk * area)
        across = row_taps[v : v + chunk].transpose(1, 0, 2).reshape(1, wide, chunk * area)
        sheet = (down * across).astype(jnp.bfloat16)
        sheets.append(sheet.reshape(tall * wide, chunk * area))
    own, _ = lax.optimization_barrier((own, sheets))
    above, below = from_sides(own, own, "gz")
    own = jnp.concatenate([above, own, below], axis=0)
    blocks, near = [], []
    for c in range(chunks):
        blocks.append(
            join(c, ends, usual_table[1], late_cell, arrived, late, gz_count, chunk * positions)
        )
        near.append(ring_step(blocks[c][gz_count // 2], blocks[c][gz_count // 2 + 1]))
        near[c], arrived = lax.optimization_barrier((near[c], arrived))
    joined = [ring_sum(blocks[c], *near[c]) for c in range(chunks)]
    own, column_kernels, _ = lax.optimization_barrier((own, kernels[:, 2], blocks[-1][0]))
    above, below = from_sides(own, own, "gy")
    own = jnp.concatenate([above, own, below], axis=1)
    own = own.reshape(tall * wide, cols)
    column = jnp.concatenate(
        [jnp.arange(cols), jnp.arange(-side, 0), jnp.arange(cols, cols + side)]
        + [jnp.full(cols - 2 * side, -cols)]
    )
    offset = column[:, None] - jnp.arange(cols)[None, :]
    col_taps = taps_table(column_kernels, radius + offset).astype(jnp.bfloat16)
    col_taps_back = taps_table(column_kernels, radius - offset).astype(jnp.bfloat16)
    field = with_columns(own, side)
    total = jnp.zeros((tall * wide, cols), jnp.float32)
    for c in range(chunks):
        views = slice(c * chunk, (c + 1) * chunk)
        swept = lax.dot_general(
            sheets[c], field, (((0,), (0,)), ((), ())), preferred_element_type=jnp.float32
        )
        swept = swept.astype(jnp.bfloat16).reshape(chunk, area, -1)
        blurred = jnp.einsum(
            "vac,vck->vak", swept, col_taps[views], preferred_element_type=jnp.float32
        )
        ratio = joined[c].reshape(chunk, area, cols) / (blurred + background_level)
        ratio = ratio.astype(jnp.bfloat16).reshape(chunk * area, cols)
        ratio = with_columns(ratio, side).reshape(chunk, area, -1)
        spread = jnp.einsum(
            "vac,vck->vak", ratio, col_taps_back[views], preferred_element_type=jnp.float32
        )
        spread = spread.astype(jnp.bfloat16).reshape(chunk * area, cols)
        total = total + jnp.dot(sheets[c], spread, preferred_element_type=jnp.float32)
    total = total.reshape(tall, wide, cols)
    first, second = neighbours(
        total[side + depth :].astype(jnp.float16), total[:side].astype(jnp.float16), "gz"
    )
    total = total[side : side + depth] + first.astype(jnp.float32) + second.astype(jnp.float32)
    first, second = neighbours(
        total[:, side + rows :].astype(jnp.float16), total[:, :side].astype(jnp.float16), "gy"
    )
    result = total[:, side : side + rows] + first.astype(jnp.float32) + second.astype(jnp.float32)
    return estimate * result / view_count


def solution(mesh):
    placed = (P(None, ("gz", "gy"), None, None, "gx"), P(), P(), P("gz", "gy", "gx"))
    return jax.shard_map(
        on_device, mesh=mesh, in_specs=placed, out_specs=P("gz", "gy", "gx"), check_vma=False
    )
```

```python
import functools

import jax
import jax.numpy as jnp
from jax import lax
from jax.experimental import pallas as pl
from jax.experimental.pallas import tpu as pltpu
from jax.sharding import PartitionSpec as P

background_level = 0.1
highest = lax.Precision.HIGHEST
capacity = 2
usual_slots = 56
smem = pl.BlockSpec(memory_space=pltpu.SMEM)
vmem = pl.BlockSpec(memory_space=pltpu.VMEM)


def neighbours(upward, downward, axis):
    devices = lax.axis_size(axis)
    even = lax.axis_index(axis) % 2 == 0
    first = jnp.where(even, upward, downward)
    second = jnp.where(even, downward, upward)
    bonds = [(i, i + 1) for i in range(devices - 1)]
    pairs = [[p for i, j in bonds[odd::2] for p in ((i, j), (j, i))] for odd in (0, 1)]
    return lax.ppermute(first, axis, pairs[0]), lax.ppermute(second, axis, pairs[1])


def order_sides(first, second, axis):
    even = lax.axis_index(axis) % 2 == 0
    return jnp.where(even, second, first), jnp.where(even, first, second)


def edges_kernel(value, last, first):
    rows, cols = last.shape
    groups = value.shape[0] // rows
    side = cols // groups
    group_of = lax.broadcasted_iota(jnp.int32, (rows, cols), 1) // side
    lasts = firsts = jnp.zeros((rows, cols), jnp.float32)
    for g in range(groups):
        block = value[g * rows : (g + 1) * rows].astype(jnp.float32)
        lasts = jnp.where(group_of == g, pltpu.roll(block, (g + 1) * side % cols, 1), lasts)
        firsts = jnp.where(group_of == g, pltpu.roll(block, g * side, 1), firsts)
    last[...] = lasts.astype(last.dtype)
    first[...] = firsts.astype(first.dtype)


def widen_kernel(value, before, after, wide):
    rows, cols = before.shape
    groups = value.shape[0] // rows
    side = cols // groups
    lane = lax.broadcasted_iota(jnp.int32, (rows, cols), 1)
    befores, afters = before[...].astype(jnp.float32), after[...].astype(jnp.float32)
    for g in range(groups):
        part = slice(g * rows, (g + 1) * rows)
        left = pltpu.roll(befores, (cols - g * side) % cols, 1)
        right = pltpu.roll(afters, (cols + side - g * side) % cols, 1)
        halo = jnp.where(lane < side, left, jnp.where(lane < 2 * side, right, 0.0))
        wide[part, :cols] = value[part]
        wide[part, cols:] = halo.astype(wide.dtype)


def with_columns(value, side):
    rows, cols = value.shape
    groups = cols // side
    packed = jax.ShapeDtypeStruct((rows // groups, cols), value.dtype)
    last, first = pl.pallas_call(
        edges_kernel,
        out_shape=[packed, packed],
        in_specs=[vmem],
        out_specs=[vmem, vmem],
        compiler_params=pltpu.CompilerParams(vmem_limit_bytes=32 << 20),
        name="edges",
    )(value)
    before, after = order_sides(*neighbours(last, first, "gx"), "gx")
    return pl.pallas_call(
        widen_kernel,
        out_shape=jax.ShapeDtypeStruct((rows, 2 * cols), value.dtype),
        in_specs=[vmem] * 3,
        out_specs=vmem,
        compiler_params=pltpu.CompilerParams(vmem_limit_bytes=32 << 20),
        name="widen",
    )(value, before, after)


def taps_table(kernel_set, offset):
    taps = kernel_set.shape[-1]
    table = (offset[:, :, None] == jnp.arange(taps)[None, None, :]).astype(jnp.float32)
    return jnp.einsum("eim,vm->vei", table, kernel_set, precision=highest)


def slot_tables(tile_place, positions, chunks, usual):
    view_count = tile_place.shape[0]
    gz_count, gy_count = lax.axis_size("gz"), lax.axis_size("gy")
    my_gz, my_gy = lax.axis_index("gz"), lax.axis_index("gy")
    chunk = view_count // chunks
    placed = tile_place.reshape(view_count, gz_count, gy_count, -1)
    slot_count = placed.shape[-1]
    entries = view_count * slot_count
    group = lax.dynamic_index_in_dim(placed, my_gz, 1, keepdims=False)
    group = group.transpose(1, 0, 2).reshape(gy_count, entries)
    destination = group // positions
    dest_gy = destination % gy_count
    ahead = (destination // gy_count - my_gz) % gz_count
    view = jnp.arange(entries) // slot_count % chunk
    cell = (ahead * chunk + view) * positions + group % positions
    own_dest = lax.dynamic_index_in_dim(dest_gy, my_gy, 0, keepdims=True)
    sends = own_dest == jnp.arange(gy_count)[:, None]
    takes = dest_gy == my_gy
    number = jnp.broadcast_to(jnp.arange(entries)[None, :], takes.shape)
    chosen = jnp.stack([sends, takes])
    value = jnp.stack([number, cell])
    upto = (jnp.arange(entries)[:, None] <= jnp.arange(entries)[None, :]).astype(jnp.bfloat16)
    rank = jnp.dot(chosen.astype(jnp.bfloat16), upto, preferred_element_type=jnp.float32)
    rank = jnp.where(chosen, rank.astype(jnp.int32) - 1, -1)

    def table(first, lanes):
        hit = rank[..., None, :] == first + jnp.arange(lanes)[:, None]
        return jnp.sum(jnp.where(hit, value[..., None, :], 0), axis=-1).astype(jnp.int32)

    ends = [
        jnp.sum(takes[:, : c * chunk * slot_count], axis=-1).astype(jnp.int32)
        for c in range(chunks + 1)
    ]
    return table, jnp.stack(ends)


def most_slots(tile_place, positions):
    gy_count = lax.axis_size("gy")
    route_count = lax.axis_size(("gz", "gy"))
    dest_gy = (tile_place // positions) % gy_count
    dest_gy = dest_gy.reshape(tile_place.shape[0], route_count, 1, -1)
    return jnp.max(jnp.sum(dest_gy == jnp.arange(gy_count)[:, None], axis=(0, 3)))


def pack_kernel(source, tiles, outgoing):
    partners, lanes = outgoing.shape[:2]

    def one(partner, carry):
        for lane in range(lanes):
            outgoing[partner, lane] = tiles[source[partner, lane]]
        return carry

    lax.fori_loop(0, partners, one, 0)


def join_kernel(chunk, ends, cell, late_cell, arrived, late, *blocks_and_total):
    blocks, total = blocks_and_total[:-1], blocks_and_total[-1]
    partners, usual = arrived.shape[:2]
    step = 16

    def clear(index, carry):
        total[pl.ds(index * step, step)] = jnp.zeros((step,) + total.shape[1:], total.dtype)
        return carry

    lax.fori_loop(0, total.shape[0] // step, clear, 0)

    def add(cells, tiles, partner, lane):
        place = cells[partner, lane]
        total[place] = add_rounded(total[place], tiles[partner, lane])

    for partner in range(partners):
        first, last = ends[chunk, partner], ends[chunk + 1, partner]

        def add_usual(lane, carry):
            add(cell, arrived, partner, lane)
            return carry

        def add_late(lane, carry):
            add(late_cell, late, partner, lane - usual)
            return carry

        lax.fori_loop(jnp.minimum(first, usual), jnp.minimum(last, usual), add_usual, 0)
        lax.fori_loop(jnp.maximum(first, usual), jnp.maximum(last, usual), add_late, 0)
    start = 0
    for block in blocks:
        block[...] = total[start : start + block.shape[0]]
        start += block.shape[0]


def pack(source, tiles):
    return pl.pallas_call(
        pack_kernel,
        out_shape=jax.ShapeDtypeStruct(source.shape + tiles.shape[1:], tiles.dtype),
        in_specs=[smem, vmem],
        out_specs=vmem,
        compiler_params=pltpu.CompilerParams(vmem_limit_bytes=32 << 20),
        name="pack",
    )(source, tiles)


def join(chunk, ends, cell, late_cell, arrived, late, devices, cells):
    tile = arrived.shape[2:]
    half = devices // 2
    sizes = [cells] * half + [cells // 2] * 2 + [cells] * (half - 1)
    return pl.pallas_call(
        functools.partial(join_kernel, chunk),
        out_shape=[jax.ShapeDtypeStruct((size,) + tile, arrived.dtype) for size in sizes],
        in_specs=[smem, smem, smem, vmem, vmem],
        out_specs=[vmem] * len(sizes),
        scratch_shapes=[pltpu.VMEM((devices * cells,) + tile, arrived.dtype)],
        compiler_params=pltpu.CompilerParams(vmem_limit_bytes=32 << 20),
        name="join",
    )(ends, cell, late_cell, arrived, late)


def unwritten(shape, dtype):
    return pl.pallas_call(
        lambda out: None,
        out_shape=jax.ShapeDtypeStruct(shape, dtype),
        out_specs=pl.BlockSpec(memory_space=pl.ANY),
        name="unwritten",
    )()


def exchange(value):
    return lax.all_to_all(value, "gy", split_axis=0, concat_axis=0, tiled=True)


def add_rounded(left, right):
    return (left.astype(jnp.float32) + right.astype(jnp.float32)).astype(left.dtype)


def ring_step(upward, downward):
    devices = lax.axis_size("gz")
    up = [(i, (i + 1) % devices) for i in range(devices)]
    down = [(j, i) for i, j in up]
    return lax.ppermute(upward, "gz", up), lax.ppermute(downward, "gz", down)


def ring_sum(blocks):
    devices = len(blocks) - 1
    half = devices // 2
    from_below, from_above = ring_step(blocks[half], blocks[half + 1])
    middle = blocks[half].shape[0]
    for ahead in range(half - 1, 0, -1):
        upward, downward = blocks[ahead], blocks[devices - ahead + 1]
        if ahead == half - 1:
            upward = jnp.concatenate([add_rounded(upward[:middle], from_below), upward[middle:]])
            downward = jnp.concatenate(
                [downward[:middle], add_rounded(downward[middle:], from_above)]
            )
        else:
            upward = add_rounded(upward, from_below)
            downward = add_rounded(downward, from_above)
        from_below, from_above = ring_step(upward, downward)
    return (
        blocks[0].astype(jnp.float32)
        + from_below.astype(jnp.float32)
        + from_above.astype(jnp.float32)
    )


def on_device(recorded, tile_place, psf, estimate):
    view_count = recorded.shape[0]
    tile_depth, tile_rows = recorded.shape[2:4]
    depth, rows, cols = estimate.shape
    per_row = rows // tile_rows
    positions = depth // tile_depth * per_row
    area = depth * rows
    radius = (psf.shape[2] - 1) // 2
    side = 16
    tall, wide = depth + 2 * side, rows + 2 * side
    chunks = 2
    chunk = view_count // chunks
    gz_count, gy_count = lax.axis_size("gz"), lax.axis_size("gy")
    tiles = recorded.reshape(-1, tile_depth * tile_rows, cols)
    lanes = gz_count * capacity * view_count
    usual = min(usual_slots, lanes)
    own = estimate.astype(jnp.bfloat16)
    own_rows = neighbours(own, own, "gy")
    table, ends = slot_tables(tile_place, positions, chunks, usual)
    usual_table = table(0, usual)

    def late_exchange():
        late_table = table(usual, lanes - usual)
        return exchange(pack(late_table[0], tiles)), late_table[1]

    def no_exchange():
        shape = (gy_count, lanes - usual)
        return unwritten(shape + tiles.shape[1:], tiles.dtype), jnp.zeros(shape, jnp.int32)

    late, late_cell = lax.cond(
        most_slots(tile_place, positions) > usual, late_exchange, no_exchange
    )
    usual_table, late_cell = lax.optimization_barrier((usual_table, late_cell))
    outgoing = pack(usual_table[0], tiles)
    outgoing, psf, own_rows = lax.optimization_barrier((outgoing, psf, own_rows))
    arrived = exchange(outgoing)

    kernels = psf / jnp.sum(psf, axis=-1, keepdims=True)
    line = jnp.arange(area)
    place, inside = line // (tile_depth * tile_rows), line % (tile_depth * tile_rows)
    line_depth = place // per_row * tile_depth + inside // tile_rows
    line_row = place % per_row * tile_rows + inside % tile_rows
    reach = radius - side
    depth_taps = taps_table(kernels[:, 0], jnp.arange(tall)[:, None] - line_depth[None, :] + reach)
    row_taps = taps_table(kernels[:, 1], jnp.arange(wide)[:, None] - line_row[None, :] + reach)
    sheets = []
    for v in range(0, view_count, chunk):
        down = depth_taps[v : v + chunk].transpose(1, 0, 2).reshape(tall, 1, chunk * area)
        across = row_taps[v : v + chunk].transpose(1, 0, 2).reshape(1, wide, chunk * area)
        sheet = (down * across).astype(jnp.bfloat16)
        sheets.append(sheet.reshape(tall * wide, chunk * area))
    above, below = order_sides(*own_rows, "gy")
    own = jnp.concatenate([above, own, below], axis=1)
    above, below = order_sides(*neighbours(own, own, "gz"), "gz")
    own = jnp.concatenate([above, own, below], axis=0)
    own = own.reshape(tall * wide, cols)
    column = jnp.concatenate(
        [jnp.arange(cols), jnp.arange(-side, 0), jnp.arange(cols, cols + side)]
        + [jnp.full(cols - 2 * side, -cols)]
    )
    offset = column[:, None] - jnp.arange(cols)[None, :]
    col_taps = taps_table(kernels[:, 2], radius + offset).astype(jnp.bfloat16)
    col_taps_back = taps_table(kernels[:, 2], radius - offset).astype(jnp.bfloat16)
    field = with_columns(own, side)
    blurred = []
    for c in range(chunks):
        swept = lax.dot_general(
            sheets[c], field, (((0,), (0,)), ((), ())), preferred_element_type=jnp.float32
        )
        swept = swept.astype(jnp.bfloat16).reshape(chunk, area, -1)
        blurred.append(
            jnp.einsum(
                "vac,vck->vak",
                swept,
                col_taps[c * chunk : (c + 1) * chunk],
                preferred_element_type=jnp.float32,
            )
        )
    arrived, blurred = lax.optimization_barrier((arrived, blurred))
    joined = []
    for c in range(chunks):
        blocks = join(c, ends, usual_table[1], late_cell, arrived, late, gz_count, chunk * positions)
        joined.append(ring_sum(blocks))
    total = jnp.zeros((tall * wide, cols), jnp.float32)
    for c in range(chunks):
        views = slice(c * chunk, (c + 1) * chunk)
        ratio = joined[c].reshape(chunk, area, cols) / (blurred[c] + background_level)
        ratio = ratio.astype(jnp.bfloat16).reshape(chunk * area, cols)
        ratio = with_columns(ratio, side).reshape(chunk, area, -1)
        spread = jnp.einsum(
            "vac,vck->vak", ratio, col_taps_back[views], preferred_element_type=jnp.float32
        )
        spread = spread.astype(jnp.bfloat16).reshape(chunk * area, cols)
        total = total + jnp.dot(sheets[c], spread, preferred_element_type=jnp.float32)
    total = total.reshape(tall, wide, cols)
    first, second = neighbours(
        total[side + depth :].astype(jnp.float16), total[:side].astype(jnp.float16), "gz"
    )
    total = total[side : side + depth] + first.astype(jnp.float32) + second.astype(jnp.float32)
    first, second = neighbours(
        total[:, side + rows :].astype(jnp.float16), total[:, :side].astype(jnp.float16), "gy"
    )
    result = total[:, side : side + rows] + first.astype(jnp.float32) + second.astype(jnp.float32)
    return estimate * result / view_count


def solution(mesh):
    placed = (P(None, ("gz", "gy"), None, None, "gx"), P(), P(), P("gz", "gy", "gx"))
    return jax.shard_map(
        on_device, mesh=mesh, in_specs=placed, out_specs=P("gz", "gy", "gx"), check_vma=False
    )
```

```python
import functools

import jax
import jax.numpy as jnp
from jax import lax
from jax.experimental import pallas as pl
from jax.experimental.pallas import tpu as pltpu
from jax.sharding import PartitionSpec as P

background_level = 0.1
highest = lax.Precision.HIGHEST
capacity = 2
usual_slots = 56
smem = pl.BlockSpec(memory_space=pltpu.SMEM)
vmem = pl.BlockSpec(memory_space=pltpu.VMEM)


def neighbours(upward, downward, axis):
    devices = lax.axis_size(axis)
    even = lax.axis_index(axis) % 2 == 0
    first = jnp.where(even, upward, downward)
    second = jnp.where(even, downward, upward)
    bonds = [(i, i + 1) for i in range(devices - 1)]
    pairs = [[p for i, j in bonds[odd::2] for p in ((i, j), (j, i))] for odd in (0, 1)]
    return lax.ppermute(first, axis, pairs[0]), lax.ppermute(second, axis, pairs[1])


def order_sides(first, second, axis):
    even = lax.axis_index(axis) % 2 == 0
    return jnp.where(even, second, first), jnp.where(even, first, second)


def edges_kernel(value, last, first):
    rows, cols = last.shape
    groups = value.shape[0] // rows
    side = cols // groups
    group_of = lax.broadcasted_iota(jnp.int32, (rows, cols), 1) // side
    lasts = firsts = jnp.zeros((rows, cols), jnp.float32)
    for g in range(groups):
        block = value[g * rows : (g + 1) * rows].astype(jnp.float32)
        lasts = jnp.where(group_of == g, pltpu.roll(block, (g + 1) * side % cols, 1), lasts)
        firsts = jnp.where(group_of == g, pltpu.roll(block, g * side, 1), firsts)
    last[...] = lasts.astype(last.dtype)
    first[...] = firsts.astype(first.dtype)


def widen_kernel(value, before, after, wide):
    rows, cols = before.shape
    groups = value.shape[0] // rows
    side = cols // groups
    lane = lax.broadcasted_iota(jnp.int32, (rows, cols), 1)
    befores, afters = before[...].astype(jnp.float32), after[...].astype(jnp.float32)
    for g in range(groups):
        part = slice(g * rows, (g + 1) * rows)
        left = pltpu.roll(befores, (cols - g * side) % cols, 1)
        right = pltpu.roll(afters, (cols + side - g * side) % cols, 1)
        halo = jnp.where(lane < side, left, jnp.where(lane < 2 * side, right, 0.0))
        wide[part, :cols] = value[part]
        wide[part, cols:] = halo.astype(wide.dtype)


def column_sides(value, side):
    rows, cols = value.shape
    groups = cols // side
    packed = jax.ShapeDtypeStruct((rows // groups, cols), value.dtype)
    last, first = pl.pallas_call(
        edges_kernel,
        out_shape=[packed, packed],
        in_specs=[vmem],
        out_specs=[vmem, vmem],
        compiler_params=pltpu.CompilerParams(vmem_limit_bytes=32 << 20),
        name="edges",
    )(value)
    return order_sides(*neighbours(last, first, "gx"), "gx")


def with_columns(value, before, after):
    rows, cols = value.shape
    return pl.pallas_call(
        widen_kernel,
        out_shape=jax.ShapeDtypeStruct((rows, 2 * cols), value.dtype),
        in_specs=[vmem] * 3,
        out_specs=vmem,
        compiler_params=pltpu.CompilerParams(vmem_limit_bytes=32 << 20),
        name="widen",
    )(value, before, after)


def taps_table(kernel_set, offset):
    taps = kernel_set.shape[-1]
    table = (offset[:, :, None] == jnp.arange(taps)[None, None, :]).astype(jnp.float32)
    return jnp.einsum("eim,vm->vei", table, kernel_set, precision=highest)


def slot_tables(tile_place, positions, chunks, usual):
    view_count = tile_place.shape[0]
    gz_count, gy_count = lax.axis_size("gz"), lax.axis_size("gy")
    my_gz, my_gy = lax.axis_index("gz"), lax.axis_index("gy")
    chunk = view_count // chunks
    placed = tile_place.reshape(view_count, gz_count, gy_count, -1)
    slot_count = placed.shape[-1]
    entries = view_count * slot_count
    group = lax.dynamic_index_in_dim(placed, my_gz, 1, keepdims=False)
    group = group.transpose(1, 0, 2).reshape(gy_count, entries)
    destination = group // positions
    dest_gy = destination % gy_count
    ahead = (destination // gy_count - my_gz) % gz_count
    view = jnp.arange(entries) // slot_count % chunk
    cell = (ahead * chunk + view) * positions + group % positions
    own_dest = lax.dynamic_index_in_dim(dest_gy, my_gy, 0, keepdims=True)
    sends = own_dest == jnp.arange(gy_count)[:, None]
    takes = dest_gy == my_gy
    number = jnp.broadcast_to(jnp.arange(entries)[None, :], takes.shape)
    chosen = jnp.stack([sends, takes])
    value = jnp.stack([number, cell])
    upto = (jnp.arange(entries)[:, None] <= jnp.arange(entries)[None, :]).astype(jnp.bfloat16)
    rank = jnp.dot(chosen.astype(jnp.bfloat16), upto, preferred_element_type=jnp.float32)
    rank = jnp.where(chosen, rank.astype(jnp.int32) - 1, -1)

    def table(first, lanes):
        hit = rank[..., None, :] == first + jnp.arange(lanes)[:, None]
        return jnp.sum(jnp.where(hit, value[..., None, :], 0), axis=-1).astype(jnp.int32)

    ends = [
        jnp.sum(takes[:, : c * chunk * slot_count], axis=-1).astype(jnp.int32)
        for c in range(chunks + 1)
    ]
    return table, jnp.stack(ends)


def most_slots(tile_place, positions):
    gy_count = lax.axis_size("gy")
    route_count = lax.axis_size(("gz", "gy"))
    dest_gy = (tile_place // positions) % gy_count
    dest_gy = dest_gy.reshape(tile_place.shape[0], route_count, 1, -1)
    return jnp.max(jnp.sum(dest_gy == jnp.arange(gy_count)[:, None], axis=(0, 3)))


def pack_kernel(source, tiles, outgoing, filled, done):
    partners, lanes = filled.shape[:2]
    copies = []
    for partner in range(partners):

        def fill(index, carry):
            for lane in range(8):
                lane = index * 8 + lane
                filled[partner, lane] = tiles[source[partner, lane]]
            return carry

        lax.fori_loop(0, lanes // 8, fill, 0)
        copy = pltpu.make_async_copy(filled.at[partner], outgoing.at[partner], done.at[partner])
        copy.start()
        copies.append(copy)
    for copy in copies:
        copy.wait()


def join_kernel(chunk, ends, cell, late_cell, arrived, late, *blocks_and_total):
    blocks, total = blocks_and_total[:-1], blocks_and_total[-1]
    partners, usual = arrived.shape[:2]
    step = 16

    def clear(index, carry):
        total[pl.ds(index * step, step)] = jnp.zeros((step,) + total.shape[1:], total.dtype)
        return carry

    lax.fori_loop(0, total.shape[0] // step, clear, 0)

    def add(cells, tiles, partner, lane):
        place = cells[partner, lane]
        total[place] = add_rounded(total[place], tiles[partner, lane])

    for partner in range(partners):
        first, last = ends[chunk, partner], ends[chunk + 1, partner]

        def add_usual(lane, carry):
            add(cell, arrived, partner, lane)
            return carry

        def add_late(lane, carry):
            add(late_cell, late, partner, lane - usual)
            return carry

        lax.fori_loop(jnp.minimum(first, usual), jnp.minimum(last, usual), add_usual, 0)
        lax.fori_loop(jnp.maximum(first, usual), jnp.maximum(last, usual), add_late, 0)
    start = 0
    for block in blocks:
        block[...] = total[start : start + block.shape[0]]
        start += block.shape[0]


def pack(source, tiles):
    shape = source.shape + tiles.shape[1:]
    return pl.pallas_call(
        pack_kernel,
        out_shape=jax.ShapeDtypeStruct(shape, tiles.dtype),
        in_specs=[smem, vmem],
        out_specs=pl.BlockSpec(memory_space=pl.ANY),
        scratch_shapes=[
            pltpu.VMEM(shape, tiles.dtype),
            pltpu.SemaphoreType.DMA((source.shape[0],)),
        ],
        compiler_params=pltpu.CompilerParams(vmem_limit_bytes=32 << 20),
        name="pack",
    )(source, tiles)


def join(chunk, ends, cell, late_cell, arrived, late, devices, cells):
    tile = arrived.shape[2:]
    half = devices // 2
    sizes = [cells] * half + [cells // 2] * 2 + [cells] * (half - 1)
    return pl.pallas_call(
        functools.partial(join_kernel, chunk),
        out_shape=[jax.ShapeDtypeStruct((size,) + tile, arrived.dtype) for size in sizes],
        in_specs=[smem, smem, smem, vmem, vmem],
        out_specs=[vmem] * len(sizes),
        scratch_shapes=[pltpu.VMEM((devices * cells,) + tile, arrived.dtype)],
        compiler_params=pltpu.CompilerParams(vmem_limit_bytes=32 << 20),
        name="join",
    )(ends, cell, late_cell, arrived, late)


def unwritten(shape, dtype):
    return pl.pallas_call(
        lambda out: None,
        out_shape=jax.ShapeDtypeStruct(shape, dtype),
        out_specs=pl.BlockSpec(memory_space=pl.ANY),
        name="unwritten",
    )()


def exchange(value):
    return lax.all_to_all(value, "gy", split_axis=0, concat_axis=0, tiled=True)


def add_rounded(left, right):
    return (left.astype(jnp.float32) + right.astype(jnp.float32)).astype(left.dtype)


def ring_step(upward, downward):
    devices = lax.axis_size("gz")
    up = [(i, (i + 1) % devices) for i in range(devices)]
    down = [(j, i) for i, j in up]
    return lax.ppermute(upward, "gz", up), lax.ppermute(downward, "gz", down)


def ring_sum(blocks):
    devices = len(blocks) - 1
    half = devices // 2
    from_below, from_above = ring_step(blocks[half], blocks[half + 1])
    middle = blocks[half].shape[0]
    for ahead in range(half - 1, 0, -1):
        upward, downward = blocks[ahead], blocks[devices - ahead + 1]
        if ahead == half - 1:
            upward = jnp.concatenate([add_rounded(upward[:middle], from_below), upward[middle:]])
            downward = jnp.concatenate(
                [downward[:middle], add_rounded(downward[middle:], from_above)]
            )
        else:
            upward = add_rounded(upward, from_below)
            downward = add_rounded(downward, from_above)
        from_below, from_above = ring_step(upward, downward)
    return (
        blocks[0].astype(jnp.float32)
        + from_below.astype(jnp.float32)
        + from_above.astype(jnp.float32)
    )


def on_device(recorded, tile_place, psf, estimate):
    view_count = recorded.shape[0]
    tile_depth, tile_rows = recorded.shape[2:4]
    depth, rows, cols = estimate.shape
    per_row = rows // tile_rows
    positions = depth // tile_depth * per_row
    area = depth * rows
    radius = (psf.shape[2] - 1) // 2
    side = 16
    tall, wide = depth + 2 * side, rows + 2 * side
    chunks = 2
    chunk = view_count // chunks
    gz_count, gy_count = lax.axis_size("gz"), lax.axis_size("gy")
    tiles = recorded.reshape(-1, tile_depth * tile_rows, cols)
    lanes = gz_count * capacity * view_count
    usual = min(usual_slots, lanes)
    own = estimate.astype(jnp.bfloat16)
    own_rows = neighbours(own, own, "gy")
    table, ends = slot_tables(tile_place, positions, chunks, usual)
    usual_table = table(0, usual)

    def late_exchange():
        late_table = table(usual, lanes - usual)
        return exchange(pack(late_table[0], tiles)), late_table[1]

    def no_exchange():
        shape = (gy_count, lanes - usual)
        return unwritten(shape + tiles.shape[1:], tiles.dtype), jnp.zeros(shape, jnp.int32)

    late, late_cell = lax.cond(
        most_slots(tile_place, positions) > usual, late_exchange, no_exchange
    )
    usual_table, late_cell = lax.optimization_barrier((usual_table, late_cell))
    outgoing = pack(usual_table[0], tiles)
    outgoing, psf, own_rows = lax.optimization_barrier((outgoing, psf, own_rows))
    arrived = exchange(outgoing)

    kernels = psf / jnp.sum(psf, axis=-1, keepdims=True)
    line = jnp.arange(area)
    place, inside = line // (tile_depth * tile_rows), line % (tile_depth * tile_rows)
    line_depth = place // per_row * tile_depth + inside // tile_rows
    line_row = place % per_row * tile_rows + inside % tile_rows
    reach = radius - side
    depth_taps = taps_table(kernels[:, 0], jnp.arange(tall)[:, None] - line_depth[None, :] + reach)
    row_taps = taps_table(kernels[:, 1], jnp.arange(wide)[:, None] - line_row[None, :] + reach)
    sheets = []
    for v in range(0, view_count, chunk):
        down = depth_taps[v : v + chunk].transpose(1, 0, 2).reshape(tall, 1, chunk * area)
        across = row_taps[v : v + chunk].transpose(1, 0, 2).reshape(1, wide, chunk * area)
        sheet = (down * across).astype(jnp.bfloat16)
        sheets.append(sheet.reshape(tall * wide, chunk * area))
    own_rows, _ = lax.optimization_barrier((own_rows, sheets))
    above, below = order_sides(*own_rows, "gy")
    own = jnp.concatenate([above, own, below], axis=1)
    above, below = order_sides(*neighbours(own, own, "gz"), "gz")
    own = jnp.concatenate([above, own, below], axis=0)
    own = own.reshape(tall * wide, cols)
    column = jnp.concatenate(
        [jnp.arange(cols), jnp.arange(-side, 0), jnp.arange(cols, cols + side)]
        + [jnp.full(cols - 2 * side, -cols)]
    )
    offset = column[:, None] - jnp.arange(cols)[None, :]
    col_taps = taps_table(kernels[:, 2], radius + offset).astype(jnp.bfloat16)
    col_taps_back = taps_table(kernels[:, 2], radius - offset).astype(jnp.bfloat16)
    before, after = column_sides(own, side)
    blocks = [
        join(c, ends, usual_table[1], late_cell, arrived, late, gz_count, chunk * positions)
        for c in range(chunks)
    ]
    own, before, after, _ = lax.optimization_barrier((own, before, after, blocks[-1][0]))
    field = with_columns(own, before, after)
    blurred = []
    for c in range(chunks):
        swept = lax.dot_general(
            sheets[c], field, (((0,), (0,)), ((), ())), preferred_element_type=jnp.float32
        )
        swept = swept.astype(jnp.bfloat16).reshape(chunk, area, -1)
        blurred.append(
            jnp.einsum(
                "vac,vck->vak",
                swept,
                col_taps[c * chunk : (c + 1) * chunk],
                preferred_element_type=jnp.float32,
            )
        )
    joined = [ring_sum(blocks[c]) for c in range(chunks)]
    total = jnp.zeros((tall * wide, cols), jnp.float32)
    for c in range(chunks):
        views = slice(c * chunk, (c + 1) * chunk)
        ratio = joined[c].reshape(chunk, area, cols) / (blurred[c] + background_level)
        ratio = ratio.astype(jnp.bfloat16).reshape(chunk * area, cols)
        ratio = with_columns(ratio, *column_sides(ratio, side)).reshape(chunk, area, -1)
        spread = jnp.einsum(
            "vac,vck->vak", ratio, col_taps_back[views], preferred_element_type=jnp.float32
        )
        spread = spread.astype(jnp.bfloat16).reshape(chunk * area, cols)
        total = total + jnp.dot(sheets[c], spread, preferred_element_type=jnp.float32)
    total = total.reshape(tall, wide, cols)
    first, second = neighbours(
        total[side + depth :].astype(jnp.float16), total[:side].astype(jnp.float16), "gz"
    )
    total = total[side : side + depth] + first.astype(jnp.float32) + second.astype(jnp.float32)
    first, second = neighbours(
        total[:, side + rows :].astype(jnp.float16), total[:, :side].astype(jnp.float16), "gy"
    )
    result = total[:, side : side + rows] + first.astype(jnp.float32) + second.astype(jnp.float32)
    return estimate * result / view_count


def solution(mesh):
    placed = (P(None, ("gz", "gy"), None, None, "gx"), P(), P(), P("gz", "gy", "gx"))
    return jax.shard_map(
        on_device, mesh=mesh, in_specs=placed, out_specs=P("gz", "gy", "gx"), check_vma=False
    )
```

```python
import functools

import jax
import jax.numpy as jnp
from jax import lax
from jax.experimental import pallas as pl
from jax.experimental.pallas import tpu as pltpu
from jax.sharding import PartitionSpec as P

background_level = 0.1
highest = lax.Precision.HIGHEST
capacity = 2
usual_slots = 56
smem = pl.BlockSpec(memory_space=pltpu.SMEM)
vmem = pl.BlockSpec(memory_space=pltpu.VMEM)


def neighbours(upward, downward, axis):
    devices = lax.axis_size(axis)
    even = lax.axis_index(axis) % 2 == 0
    first = jnp.where(even, upward, downward)
    second = jnp.where(even, downward, upward)
    bonds = [(i, i + 1) for i in range(devices - 1)]
    pairs = [[p for i, j in bonds[odd::2] for p in ((i, j), (j, i))] for odd in (0, 1)]
    return lax.ppermute(first, axis, pairs[0]), lax.ppermute(second, axis, pairs[1])


def from_sides(upward, downward, axis):
    even = lax.axis_index(axis) % 2 == 0
    first, second = neighbours(upward, downward, axis)
    return jnp.where(even, second, first), jnp.where(even, first, second)


def edges_kernel(value, last, first):
    rows, cols = last.shape
    groups = value.shape[0] // rows
    side = cols // groups
    group_of = lax.broadcasted_iota(jnp.int32, (rows, cols), 1) // side
    lasts = firsts = jnp.zeros((rows, cols), jnp.float32)
    for g in range(groups):
        block = value[g * rows : (g + 1) * rows].astype(jnp.float32)
        lasts = jnp.where(group_of == g, pltpu.roll(block, (g + 1) * side % cols, 1), lasts)
        firsts = jnp.where(group_of == g, pltpu.roll(block, g * side, 1), firsts)
    last[...] = lasts.astype(last.dtype)
    first[...] = firsts.astype(first.dtype)


def widen_kernel(value, before, after, wide):
    rows, cols = before.shape
    groups = value.shape[0] // rows
    side = cols // groups
    lane = lax.broadcasted_iota(jnp.int32, (rows, cols), 1)
    befores, afters = before[...].astype(jnp.float32), after[...].astype(jnp.float32)
    for g in range(groups):
        part = slice(g * rows, (g + 1) * rows)
        left = pltpu.roll(befores, (cols - g * side) % cols, 1)
        right = pltpu.roll(afters, (cols + side - g * side) % cols, 1)
        halo = jnp.where(lane < side, left, jnp.where(lane < 2 * side, right, 0.0))
        wide[part, :cols] = value[part]
        wide[part, cols:] = halo.astype(wide.dtype)


def with_columns(value, side):
    rows, cols = value.shape
    groups = cols // side
    packed = jax.ShapeDtypeStruct((rows // groups, cols), value.dtype)
    last, first = pl.pallas_call(
        edges_kernel,
        out_shape=[packed, packed],
        in_specs=[vmem],
        out_specs=[vmem, vmem],
        compiler_params=pltpu.CompilerParams(vmem_limit_bytes=32 << 20),
        name="edges",
    )(value)
    before, after = from_sides(last, first, "gx")
    return pl.pallas_call(
        widen_kernel,
        out_shape=jax.ShapeDtypeStruct((rows, 2 * cols), value.dtype),
        in_specs=[vmem] * 3,
        out_specs=vmem,
        compiler_params=pltpu.CompilerParams(vmem_limit_bytes=32 << 20),
        name="widen",
    )(value, before, after)


def taps_table(kernel_set, offset):
    taps = kernel_set.shape[-1]
    table = (offset[:, :, None] == jnp.arange(taps)[None, None, :]).astype(jnp.float32)
    return jnp.einsum("eim,vm->vei", table, kernel_set, precision=highest)


def slot_tables(tile_place, positions, chunks, usual):
    view_count = tile_place.shape[0]
    gz_count, gy_count = lax.axis_size("gz"), lax.axis_size("gy")
    my_gz, my_gy = lax.axis_index("gz"), lax.axis_index("gy")
    chunk = view_count // chunks
    placed = tile_place.reshape(view_count, gz_count, gy_count, -1)
    slot_count = placed.shape[-1]
    entries = view_count * slot_count
    group = lax.dynamic_index_in_dim(placed, my_gz, 1, keepdims=False)
    group = group.transpose(1, 0, 2).reshape(gy_count, entries)
    destination = group // positions
    dest_gy = destination % gy_count
    ahead = (destination // gy_count - my_gz) % gz_count
    view = jnp.arange(entries) // slot_count % chunk
    cell = (ahead * chunk + view) * positions + group % positions
    own_dest = lax.dynamic_index_in_dim(dest_gy, my_gy, 0, keepdims=True)
    sends = own_dest == jnp.arange(gy_count)[:, None]
    takes = dest_gy == my_gy
    number = jnp.broadcast_to(jnp.arange(entries)[None, :], takes.shape)
    chosen = jnp.stack([sends, takes])
    value = jnp.stack([number, cell])
    upto = (jnp.arange(entries)[:, None] <= jnp.arange(entries)[None, :]).astype(jnp.bfloat16)
    rank = jnp.dot(chosen.astype(jnp.bfloat16), upto, preferred_element_type=jnp.float32)
    rank = jnp.where(chosen, rank.astype(jnp.int32) - 1, -1)

    def table(first, lanes):
        hit = rank[..., None, :] == first + jnp.arange(lanes)[:, None]
        return jnp.sum(jnp.where(hit, value[..., None, :], 0), axis=-1).astype(jnp.int32)

    ends = [
        jnp.sum(takes[:, : c * chunk * slot_count], axis=-1).astype(jnp.int32)
        for c in range(chunks + 1)
    ]
    return table, jnp.stack(ends)


def most_slots(tile_place, positions):
    gy_count = lax.axis_size("gy")
    route_count = lax.axis_size(("gz", "gy"))
    dest_gy = (tile_place // positions) % gy_count
    dest_gy = dest_gy.reshape(tile_place.shape[0], route_count, 1, -1)
    return jnp.max(jnp.sum(dest_gy == jnp.arange(gy_count)[:, None], axis=(0, 3)))


def pack_kernel(source, tiles, outgoing):
    partners, lanes = outgoing.shape[:2]

    def one(partner, carry):
        for lane in range(lanes):
            outgoing[partner, lane] = tiles[source[partner, lane]]
        return carry

    lax.fori_loop(0, partners, one, 0)


def join_kernel(chunk, ends, cell, late_cell, arrived, late, *blocks_and_total):
    blocks, total = blocks_and_total[:-1], blocks_and_total[-1]
    partners, usual = arrived.shape[:2]
    step = 16

    def clear(index, carry):
        total[pl.ds(index * step, step)] = jnp.zeros((step,) + total.shape[1:], total.dtype)
        return carry

    lax.fori_loop(0, total.shape[0] // step, clear, 0)

    def add(cells, tiles, partner, lane):
        place = cells[partner, lane]
        total[place] = add_rounded(total[place], tiles[partner, lane])

    for partner in range(partners):
        first, last = ends[chunk, partner], ends[chunk + 1, partner]

        def add_usual(lane, carry):
            add(cell, arrived, partner, lane)
            return carry

        def add_late(lane, carry):
            add(late_cell, late, partner, lane - usual)
            return carry

        lax.fori_loop(jnp.minimum(first, usual), jnp.minimum(last, usual), add_usual, 0)
        lax.fori_loop(jnp.maximum(first, usual), jnp.maximum(last, usual), add_late, 0)
    start = 0
    for block in blocks:
        block[...] = total[start : start + block.shape[0]]
        start += block.shape[0]


def pack(source, tiles):
    return pl.pallas_call(
        pack_kernel,
        out_shape=jax.ShapeDtypeStruct(source.shape + tiles.shape[1:], tiles.dtype),
        in_specs=[smem, vmem],
        out_specs=vmem,
        compiler_params=pltpu.CompilerParams(vmem_limit_bytes=32 << 20),
        name="pack",
    )(source, tiles)


def join(chunk, ends, cell, late_cell, arrived, late, devices, cells):
    tile = arrived.shape[2:]
    half = devices // 2
    sizes = [cells] * half + [cells // 2] * 2 + [cells] * (half - 1)
    return pl.pallas_call(
        functools.partial(join_kernel, chunk),
        out_shape=[jax.ShapeDtypeStruct((size,) + tile, arrived.dtype) for size in sizes],
        in_specs=[smem, smem, smem, vmem, vmem],
        out_specs=[vmem] * len(sizes),
        scratch_shapes=[pltpu.VMEM((devices * cells,) + tile, arrived.dtype)],
        compiler_params=pltpu.CompilerParams(vmem_limit_bytes=32 << 20),
        name="join",
    )(ends, cell, late_cell, arrived, late)


def unwritten(shape, dtype):
    return pl.pallas_call(
        lambda out: None,
        out_shape=jax.ShapeDtypeStruct(shape, dtype),
        out_specs=pl.BlockSpec(memory_space=pl.ANY),
        name="unwritten",
    )()


def exchange(value):
    return lax.all_to_all(value, "gy", split_axis=0, concat_axis=0, tiled=True)


def add_rounded(left, right):
    return (left.astype(jnp.float32) + right.astype(jnp.float32)).astype(left.dtype)


def ring_step(upward, downward):
    devices = lax.axis_size("gz")
    up = [(i, (i + 1) % devices) for i in range(devices)]
    down = [(j, i) for i, j in up]
    return lax.ppermute(upward, "gz", up), lax.ppermute(downward, "gz", down)


def ring_sum(blocks, from_below, from_above):
    devices = len(blocks) - 1
    half = devices // 2
    middle = blocks[half].shape[0]
    for ahead in range(half - 1, 0, -1):
        upward, downward = blocks[ahead], blocks[devices - ahead + 1]
        if ahead == half - 1:
            upward = jnp.concatenate([add_rounded(upward[:middle], from_below), upward[middle:]])
            downward = jnp.concatenate(
                [downward[:middle], add_rounded(downward[middle:], from_above)]
            )
        else:
            upward = add_rounded(upward, from_below)
            downward = add_rounded(downward, from_above)
        from_below, from_above = ring_step(upward, downward)
    return (
        blocks[0].astype(jnp.float32)
        + from_below.astype(jnp.float32)
        + from_above.astype(jnp.float32)
    )


def on_device(recorded, tile_place, psf, estimate):
    view_count = recorded.shape[0]
    tile_depth, tile_rows = recorded.shape[2:4]
    depth, rows, cols = estimate.shape
    per_row = rows // tile_rows
    positions = depth // tile_depth * per_row
    area = depth * rows
    radius = (psf.shape[2] - 1) // 2
    side = 16
    tall, wide = depth + 2 * side, rows + 2 * side
    chunks = 2
    chunk = view_count // chunks
    gz_count, gy_count = lax.axis_size("gz"), lax.axis_size("gy")
    tiles = recorded.reshape(-1, tile_depth * tile_rows, cols)
    lanes = gz_count * capacity * view_count
    usual = min(usual_slots, lanes)
    table, ends = slot_tables(tile_place, positions, chunks, usual)
    usual_table = table(0, usual)

    def late_exchange():
        late_table = table(usual, lanes - usual)
        return exchange(pack(late_table[0], tiles)), late_table[1]

    def no_exchange():
        shape = (gy_count, lanes - usual)
        return unwritten(shape + tiles.shape[1:], tiles.dtype), jnp.zeros(shape, jnp.int32)

    late, late_cell = lax.cond(
        most_slots(tile_place, positions) > usual, late_exchange, no_exchange
    )
    usual_table, late_cell = lax.optimization_barrier((usual_table, late_cell))
    outgoing, psf = lax.optimization_barrier((pack(usual_table[0], tiles), psf))
    arrived = exchange(outgoing)
    own = estimate.astype(jnp.bfloat16)

    kernels = psf / jnp.sum(psf, axis=-1, keepdims=True)
    line = jnp.arange(area)
    place, inside = line // (tile_depth * tile_rows), line % (tile_depth * tile_rows)
    line_depth = place // per_row * tile_depth + inside // tile_rows
    line_row = place % per_row * tile_rows + inside % tile_rows
    reach = radius - side
    depth_taps = taps_table(kernels[:, 0], jnp.arange(tall)[:, None] - line_depth[None, :] + reach)
    row_taps = taps_table(kernels[:, 1], jnp.arange(wide)[:, None] - line_row[None, :] + reach)
    sheets = []
    for v in range(0, view_count, chunk):
        down = depth_taps[v : v + chunk].transpose(1, 0, 2).reshape(tall, 1, chunk * area)
        across = row_taps[v : v + chunk].transpose(1, 0, 2).reshape(1, wide, chunk * area)
        sheet = (down * across).astype(jnp.bfloat16)
        sheets.append(sheet.reshape(tall * wide, chunk * area))
    own, _ = lax.optimization_barrier((own, sheets))
    above, below = from_sides(own, own, "gz")
    own = jnp.concatenate([above, own, below], axis=0)
    blocks, near = [], []
    for c in range(chunks):
        blocks.append(
            join(c, ends, usual_table[1], late_cell, arrived, late, gz_count, chunk * positions)
        )
        near.append(ring_step(blocks[c][gz_count // 2], blocks[c][gz_count // 2 + 1]))
    joined = [ring_sum(blocks[c], *near[c]) for c in range(chunks)]
    own, column_kernels, _ = lax.optimization_barrier((own, kernels[:, 2], blocks[-1][0]))
    above, below = from_sides(own, own, "gy")
    own = jnp.concatenate([above, own, below], axis=1)
    own = own.reshape(tall * wide, cols)
    column = jnp.concatenate(
        [jnp.arange(cols), jnp.arange(-side, 0), jnp.arange(cols, cols + side)]
        + [jnp.full(cols - 2 * side, -cols)]
    )
    offset = column[:, None] - jnp.arange(cols)[None, :]
    col_taps = taps_table(column_kernels, radius + offset).astype(jnp.bfloat16)
    col_taps_back = taps_table(column_kernels, radius - offset).astype(jnp.bfloat16)
    field = with_columns(own, side)
    total = jnp.zeros((tall * wide, cols), jnp.float32)
    for c in range(chunks):
        views = slice(c * chunk, (c + 1) * chunk)
        swept = lax.dot_general(
            sheets[c], field, (((0,), (0,)), ((), ())), preferred_element_type=jnp.float32
        )
        swept = swept.astype(jnp.bfloat16).reshape(chunk, area, -1)
        blurred = jnp.einsum(
            "vac,vck->vak", swept, col_taps[views], preferred_element_type=jnp.float32
        )
        ratio = joined[c].reshape(chunk, area, cols) / (blurred + background_level)
        ratio = ratio.astype(jnp.bfloat16).reshape(chunk * area, cols)
        ratio = with_columns(ratio, side).reshape(chunk, area, -1)
        spread = jnp.einsum(
            "vac,vck->vak", ratio, col_taps_back[views], preferred_element_type=jnp.float32
        )
        spread = spread.astype(jnp.bfloat16).reshape(chunk * area, cols)
        total = total + jnp.dot(sheets[c], spread, preferred_element_type=jnp.float32)
    total = total.reshape(tall, wide, cols)
    first, second = neighbours(
        total[side + depth :].astype(jnp.float16), total[:side].astype(jnp.float16), "gz"
    )
    total = total[side : side + depth] + first.astype(jnp.float32) + second.astype(jnp.float32)
    first, second = neighbours(
        total[:, side + rows :].astype(jnp.float16), total[:, :side].astype(jnp.float16), "gy"
    )
    result = total[:, side : side + rows] + first.astype(jnp.float32) + second.astype(jnp.float32)
    return estimate * result / view_count


def solution(mesh):
    placed = (P(None, ("gz", "gy"), None, None, "gx"), P(), P(), P("gz", "gy", "gx"))
    return jax.shard_map(
        on_device, mesh=mesh, in_specs=placed, out_specs=P("gz", "gy", "gx"), check_vma=False
    )
```

```python
import functools

import jax
import jax.numpy as jnp
from jax import lax
from jax.experimental import pallas as pl
from jax.experimental.pallas import tpu as pltpu
from jax.sharding import PartitionSpec as P

background_level = 0.1
highest = lax.Precision.HIGHEST
capacity = 2
usual_slots = 56
smem = pl.BlockSpec(memory_space=pltpu.SMEM)
vmem = pl.BlockSpec(memory_space=pltpu.VMEM)


def neighbours(upward, downward, axis):
    devices = lax.axis_size(axis)
    even = lax.axis_index(axis) % 2 == 0
    first = jnp.where(even, upward, downward)
    second = jnp.where(even, downward, upward)
    bonds = [(i, i + 1) for i in range(devices - 1)]
    pairs = [[p for i, j in bonds[odd::2] for p in ((i, j), (j, i))] for odd in (0, 1)]
    return lax.ppermute(first, axis, pairs[0]), lax.ppermute(second, axis, pairs[1])


def order_sides(first, second, axis):
    even = lax.axis_index(axis) % 2 == 0
    return jnp.where(even, second, first), jnp.where(even, first, second)


def edges_kernel(value, last, first):
    rows, cols = last.shape
    groups = value.shape[0] // rows
    side = cols // groups
    group_of = lax.broadcasted_iota(jnp.int32, (rows, cols), 1) // side
    lasts = firsts = jnp.zeros((rows, cols), jnp.float32)
    for g in range(groups):
        block = value[g * rows : (g + 1) * rows].astype(jnp.float32)
        lasts = jnp.where(group_of == g, pltpu.roll(block, (g + 1) * side % cols, 1), lasts)
        firsts = jnp.where(group_of == g, pltpu.roll(block, g * side, 1), firsts)
    last[...] = lasts.astype(last.dtype)
    first[...] = firsts.astype(first.dtype)


def widen_kernel(value, before, after, wide):
    rows, cols = before.shape
    groups = value.shape[0] // rows
    side = cols // groups
    lane = lax.broadcasted_iota(jnp.int32, (rows, cols), 1)
    befores, afters = before[...].astype(jnp.float32), after[...].astype(jnp.float32)
    for g in range(groups):
        part = slice(g * rows, (g + 1) * rows)
        left = pltpu.roll(befores, (cols - g * side) % cols, 1)
        right = pltpu.roll(afters, (cols + side - g * side) % cols, 1)
        halo = jnp.where(lane < side, left, jnp.where(lane < 2 * side, right, 0.0))
        wide[part, :cols] = value[part]
        wide[part, cols:] = halo.astype(wide.dtype)


def with_columns(value, side):
    rows, cols = value.shape
    groups = cols // side
    packed = jax.ShapeDtypeStruct((rows // groups, cols), value.dtype)
    last, first = pl.pallas_call(
        edges_kernel,
        out_shape=[packed, packed],
        in_specs=[vmem],
        out_specs=[vmem, vmem],
        compiler_params=pltpu.CompilerParams(vmem_limit_bytes=32 << 20),
        name="edges",
    )(value)
    before, after = order_sides(*neighbours(last, first, "gx"), "gx")
    return pl.pallas_call(
        widen_kernel,
        out_shape=jax.ShapeDtypeStruct((rows, 2 * cols), value.dtype),
        in_specs=[vmem] * 3,
        out_specs=vmem,
        compiler_params=pltpu.CompilerParams(vmem_limit_bytes=32 << 20),
        name="widen",
    )(value, before, after)


def taps_table(kernel_set, offset):
    taps = kernel_set.shape[-1]
    table = (offset[:, :, None] == jnp.arange(taps)[None, None, :]).astype(jnp.float32)
    return jnp.einsum("eim,vm->vei", table, kernel_set, precision=highest)


def slot_tables(tile_place, positions, chunks, usual):
    view_count = tile_place.shape[0]
    gz_count, gy_count = lax.axis_size("gz"), lax.axis_size("gy")
    my_gz, my_gy = lax.axis_index("gz"), lax.axis_index("gy")
    chunk = view_count // chunks
    placed = tile_place.reshape(view_count, gz_count, gy_count, -1)
    slot_count = placed.shape[-1]
    entries = view_count * slot_count
    group = lax.dynamic_index_in_dim(placed, my_gz, 1, keepdims=False)
    group = group.transpose(1, 0, 2).reshape(gy_count, entries)
    destination = group // positions
    dest_gy = destination % gy_count
    ahead = (destination // gy_count - my_gz) % gz_count
    view = jnp.arange(entries) // slot_count % chunk
    cell = (ahead * chunk + view) * positions + group % positions
    own_dest = lax.dynamic_index_in_dim(dest_gy, my_gy, 0, keepdims=True)
    sends = own_dest == jnp.arange(gy_count)[:, None]
    takes = dest_gy == my_gy
    number = jnp.broadcast_to(jnp.arange(entries)[None, :], takes.shape)
    chosen = jnp.stack([sends, takes])
    value = jnp.stack([number, cell])
    upto = (jnp.arange(entries)[:, None] <= jnp.arange(entries)[None, :]).astype(jnp.bfloat16)
    rank = jnp.dot(chosen.astype(jnp.bfloat16), upto, preferred_element_type=jnp.float32)
    rank = jnp.where(chosen, rank.astype(jnp.int32) - 1, -1)

    def table(first, lanes):
        hit = rank[..., None, :] == first + jnp.arange(lanes)[:, None]
        return jnp.sum(jnp.where(hit, value[..., None, :], 0), axis=-1).astype(jnp.int32)

    ends = [
        jnp.sum(takes[:, : c * chunk * slot_count], axis=-1).astype(jnp.int32)
        for c in range(chunks + 1)
    ]
    return table, jnp.stack(ends)


def most_slots(tile_place, positions):
    gy_count = lax.axis_size("gy")
    route_count = lax.axis_size(("gz", "gy"))
    dest_gy = (tile_place // positions) % gy_count
    dest_gy = dest_gy.reshape(tile_place.shape[0], route_count, 1, -1)
    return jnp.max(jnp.sum(dest_gy == jnp.arange(gy_count)[:, None], axis=(0, 3)))


def pack_kernel(source, tiles, outgoing):
    partners, lanes = outgoing.shape[:2]

    def one(partner, carry):
        for lane in range(lanes):
            outgoing[partner, lane] = tiles[source[partner, lane]]
        return carry

    lax.fori_loop(0, partners, one, 0)


def join_kernel(chunk, ends, cell, late_cell, arrived, late, *blocks_and_total):
    blocks, total = blocks_and_total[:-1], blocks_and_total[-1]
    partners, usual = arrived.shape[:2]
    step = 16

    def clear(index, carry):
        total[pl.ds(index * step, step)] = jnp.zeros((step,) + total.shape[1:], total.dtype)
        return carry

    lax.fori_loop(0, total.shape[0] // step, clear, 0)

    def add(cells, tiles, partner, lane):
        place = cells[partner, lane]
        total[place] = add_rounded(total[place], tiles[partner, lane])

    for partner in range(partners):
        first, last = ends[chunk, partner], ends[chunk + 1, partner]

        def add_usual(lane, carry):
            add(cell, arrived, partner, lane)
            return carry

        def add_late(lane, carry):
            add(late_cell, late, partner, lane - usual)
            return carry

        lax.fori_loop(jnp.minimum(first, usual), jnp.minimum(last, usual), add_usual, 0)
        lax.fori_loop(jnp.maximum(first, usual), jnp.maximum(last, usual), add_late, 0)
    start = 0
    for block in blocks:
        block[...] = total[start : start + block.shape[0]]
        start += block.shape[0]


def pack(source, tiles):
    return pl.pallas_call(
        pack_kernel,
        out_shape=jax.ShapeDtypeStruct(source.shape + tiles.shape[1:], tiles.dtype),
        in_specs=[smem, vmem],
        out_specs=vmem,
        compiler_params=pltpu.CompilerParams(vmem_limit_bytes=32 << 20),
        name="pack",
    )(source, tiles)


def join(chunk, ends, cell, late_cell, arrived, late, devices, cells):
    tile = arrived.shape[2:]
    half = devices // 2
    sizes = [cells] * half + [cells // 2] * 2 + [cells] * (half - 1)
    return pl.pallas_call(
        functools.partial(join_kernel, chunk),
        out_shape=[jax.ShapeDtypeStruct((size,) + tile, arrived.dtype) for size in sizes],
        in_specs=[smem, smem, smem, vmem, vmem],
        out_specs=[vmem] * len(sizes),
        scratch_shapes=[pltpu.VMEM((devices * cells,) + tile, arrived.dtype)],
        compiler_params=pltpu.CompilerParams(vmem_limit_bytes=32 << 20),
        name="join",
    )(ends, cell, late_cell, arrived, late)


def unwritten(shape, dtype):
    return pl.pallas_call(
        lambda out: None,
        out_shape=jax.ShapeDtypeStruct(shape, dtype),
        out_specs=pl.BlockSpec(memory_space=pl.ANY),
        name="unwritten",
    )()


def exchange(value):
    return lax.all_to_all(value, "gy", split_axis=0, concat_axis=0, tiled=True)


def add_rounded(left, right):
    return (left.astype(jnp.float32) + right.astype(jnp.float32)).astype(left.dtype)


def ring_step(upward, downward):
    devices = lax.axis_size("gz")
    up = [(i, (i + 1) % devices) for i in range(devices)]
    down = [(j, i) for i, j in up]
    return lax.ppermute(upward, "gz", up), lax.ppermute(downward, "gz", down)


def ring_sum(blocks):
    devices = len(blocks) - 1
    half = devices // 2
    from_below, from_above = ring_step(blocks[half], blocks[half + 1])
    middle = blocks[half].shape[0]
    for ahead in range(half - 1, 0, -1):
        upward, downward = blocks[ahead], blocks[devices - ahead + 1]
        if ahead == half - 1:
            upward = jnp.concatenate([add_rounded(upward[:middle], from_below), upward[middle:]])
            downward = jnp.concatenate(
                [downward[:middle], add_rounded(downward[middle:], from_above)]
            )
        else:
            upward = add_rounded(upward, from_below)
            downward = add_rounded(downward, from_above)
        from_below, from_above = ring_step(upward, downward)
    return (
        blocks[0].astype(jnp.float32)
        + from_below.astype(jnp.float32)
        + from_above.astype(jnp.float32)
    )


def on_device(recorded, tile_place, psf, estimate):
    view_count = recorded.shape[0]
    tile_depth, tile_rows = recorded.shape[2:4]
    depth, rows, cols = estimate.shape
    per_row = rows // tile_rows
    positions = depth // tile_depth * per_row
    area = depth * rows
    radius = (psf.shape[2] - 1) // 2
    side = 16
    tall, wide = depth + 2 * side, rows + 2 * side
    chunks = 2
    chunk = view_count // chunks
    gz_count, gy_count = lax.axis_size("gz"), lax.axis_size("gy")
    tiles = recorded.reshape(-1, tile_depth * tile_rows, cols)
    lanes = gz_count * capacity * view_count
    usual = min(usual_slots, lanes)
    own = estimate.astype(jnp.bfloat16)
    own = with_columns(own.reshape(area, cols), side).reshape(depth, rows, -1)
    own_rows = neighbours(own, own, "gy")
    table, ends = slot_tables(tile_place, positions, chunks, usual)
    usual_table = table(0, usual)

    def late_exchange():
        late_table = table(usual, lanes - usual)
        return exchange(pack(late_table[0], tiles)), late_table[1]

    def no_exchange():
        shape = (gy_count, lanes - usual)
        return unwritten(shape + tiles.shape[1:], tiles.dtype), jnp.zeros(shape, jnp.int32)

    late, late_cell = lax.cond(
        most_slots(tile_place, positions) > usual, late_exchange, no_exchange
    )
    usual_table, late_cell = lax.optimization_barrier((usual_table, late_cell))
    outgoing = pack(usual_table[0], tiles)
    outgoing, psf, own_rows = lax.optimization_barrier((outgoing, psf, own_rows))
    arrived = exchange(outgoing)

    kernels = psf / jnp.sum(psf, axis=-1, keepdims=True)
    line = jnp.arange(area)
    place, inside = line // (tile_depth * tile_rows), line % (tile_depth * tile_rows)
    line_depth = place // per_row * tile_depth + inside // tile_rows
    line_row = place % per_row * tile_rows + inside % tile_rows
    reach = radius - side
    depth_taps = taps_table(kernels[:, 0], jnp.arange(tall)[:, None] - line_depth[None, :] + reach)
    row_taps = taps_table(kernels[:, 1], jnp.arange(wide)[:, None] - line_row[None, :] + reach)
    sheets = []
    for v in range(0, view_count, chunk):
        down = depth_taps[v : v + chunk].transpose(1, 0, 2).reshape(tall, 1, chunk * area)
        across = row_taps[v : v + chunk].transpose(1, 0, 2).reshape(1, wide, chunk * area)
        sheet = (down * across).astype(jnp.bfloat16)
        sheets.append(sheet.reshape(tall * wide, chunk * area))
    above, below = order_sides(*own_rows, "gy")
    own = jnp.concatenate([above, own, below], axis=1)
    above, below = order_sides(*neighbours(own, own, "gz"), "gz")
    own = jnp.concatenate([above, own, below], axis=0)
    field = own.reshape(tall * wide, -1)
    column = jnp.concatenate(
        [jnp.arange(cols), jnp.arange(-side, 0), jnp.arange(cols, cols + side)]
        + [jnp.full(cols - 2 * side, -cols)]
    )
    offset = column[:, None] - jnp.arange(cols)[None, :]
    col_taps = taps_table(kernels[:, 2], radius + offset).astype(jnp.bfloat16)
    col_taps_back = taps_table(kernels[:, 2], radius - offset).astype(jnp.bfloat16)
    blurred = []
    for c in range(chunks):
        swept = lax.dot_general(
            sheets[c], field, (((0,), (0,)), ((), ())), preferred_element_type=jnp.float32
        )
        swept = swept.astype(jnp.bfloat16).reshape(chunk, area, -1)
        blurred.append(
            jnp.einsum(
                "vac,vck->vak",
                swept,
                col_taps[c * chunk : (c + 1) * chunk],
                preferred_element_type=jnp.float32,
            )
        )
    arrived, blurred = lax.optimization_barrier((arrived, blurred))
    joined = []
    for c in range(chunks):
        blocks = join(c, ends, usual_table[1], late_cell, arrived, late, gz_count, chunk * positions)
        joined.append(ring_sum(blocks))
    total = jnp.zeros((tall * wide, cols), jnp.float32)
    for c in range(chunks):
        views = slice(c * chunk, (c + 1) * chunk)
        ratio = joined[c].reshape(chunk, area, cols) / (blurred[c] + background_level)
        ratio = ratio.astype(jnp.bfloat16).reshape(chunk * area, cols)
        ratio = with_columns(ratio, side).reshape(chunk, area, -1)
        spread = jnp.einsum(
            "vac,vck->vak", ratio, col_taps_back[views], preferred_element_type=jnp.float32
        )
        spread = spread.astype(jnp.bfloat16).reshape(chunk * area, cols)
        total = total + jnp.dot(sheets[c], spread, preferred_element_type=jnp.float32)
    total = total.reshape(tall, wide, cols)
    first, second = neighbours(
        total[side + depth :].astype(jnp.float16), total[:side].astype(jnp.float16), "gz"
    )
    total = total[side : side + depth] + first.astype(jnp.float32) + second.astype(jnp.float32)
    first, second = neighbours(
        total[:, side + rows :].astype(jnp.float16), total[:, :side].astype(jnp.float16), "gy"
    )
    result = total[:, side : side + rows] + first.astype(jnp.float32) + second.astype(jnp.float32)
    return estimate * result / view_count


def solution(mesh):
    placed = (P(None, ("gz", "gy"), None, None, "gx"), P(), P(), P("gz", "gy", "gx"))
    return jax.shard_map(
        on_device, mesh=mesh, in_specs=placed, out_specs=P("gz", "gy", "gx"), check_vma=False
    )
```

```python
import functools

import jax
import jax.numpy as jnp
from jax import lax
from jax.experimental import pallas as pl
from jax.experimental.pallas import tpu as pltpu
from jax.sharding import PartitionSpec as P

background_level = 0.1
highest = lax.Precision.HIGHEST
capacity = 2
usual_slots = 56
smem = pl.BlockSpec(memory_space=pltpu.SMEM)
vmem = pl.BlockSpec(memory_space=pltpu.VMEM)


def neighbours(upward, downward, axis):
    devices = lax.axis_size(axis)
    even = lax.axis_index(axis) % 2 == 0
    first = jnp.where(even, upward, downward)
    second = jnp.where(even, downward, upward)
    bonds = [(i, i + 1) for i in range(devices - 1)]
    pairs = [[p for i, j in bonds[odd::2] for p in ((i, j), (j, i))] for odd in (0, 1)]
    return lax.ppermute(first, axis, pairs[0]), lax.ppermute(second, axis, pairs[1])


def order_sides(first, second, axis):
    even = lax.axis_index(axis) % 2 == 0
    return jnp.where(even, second, first), jnp.where(even, first, second)


def edges_kernel(value, last, first):
    rows, cols = last.shape
    groups = value.shape[0] // rows
    side = cols // groups
    group_of = lax.broadcasted_iota(jnp.int32, (rows, cols), 1) // side
    lasts = firsts = jnp.zeros((rows, cols), jnp.float32)
    for g in range(groups):
        block = value[g * rows : (g + 1) * rows].astype(jnp.float32)
        lasts = jnp.where(group_of == g, pltpu.roll(block, (g + 1) * side % cols, 1), lasts)
        firsts = jnp.where(group_of == g, pltpu.roll(block, g * side, 1), firsts)
    last[...] = lasts.astype(last.dtype)
    first[...] = firsts.astype(first.dtype)


def widen_kernel(value, before, after, wide):
    rows, cols = before.shape
    groups = value.shape[0] // rows
    side = cols // groups
    lane = lax.broadcasted_iota(jnp.int32, (rows, cols), 1)
    befores, afters = before[...].astype(jnp.float32), after[...].astype(jnp.float32)
    for g in range(groups):
        part = slice(g * rows, (g + 1) * rows)
        left = pltpu.roll(befores, (cols - g * side) % cols, 1)
        right = pltpu.roll(afters, (cols + side - g * side) % cols, 1)
        halo = jnp.where(lane < side, left, jnp.where(lane < 2 * side, right, 0.0))
        wide[part, :cols] = value[part]
        wide[part, cols:] = halo.astype(wide.dtype)


def column_sides(value, side):
    rows, cols = value.shape
    groups = cols // side
    packed = jax.ShapeDtypeStruct((rows // groups, cols), value.dtype)
    last, first = pl.pallas_call(
        edges_kernel,
        out_shape=[packed, packed],
        in_specs=[vmem],
        out_specs=[vmem, vmem],
        compiler_params=pltpu.CompilerParams(vmem_limit_bytes=32 << 20),
        name="edges",
    )(value)
    return neighbours(last, first, "gx")


def with_columns(value, first, second):
    rows, cols = value.shape
    before, after = order_sides(first, second, "gx")
    return pl.pallas_call(
        widen_kernel,
        out_shape=jax.ShapeDtypeStruct((rows, 2 * cols), value.dtype),
        in_specs=[vmem] * 3,
        out_specs=vmem,
        compiler_params=pltpu.CompilerParams(vmem_limit_bytes=32 << 20),
        name="widen",
    )(value, before, after)


def taps_table(kernel_set, offset):
    taps = kernel_set.shape[-1]
    table = (offset[:, :, None] == jnp.arange(taps)[None, None, :]).astype(jnp.float32)
    return jnp.einsum("eim,vm->vei", table, kernel_set, precision=highest)


def slot_tables(tile_place, positions, chunks, usual):
    view_count = tile_place.shape[0]
    gz_count, gy_count = lax.axis_size("gz"), lax.axis_size("gy")
    my_gz, my_gy = lax.axis_index("gz"), lax.axis_index("gy")
    chunk = view_count // chunks
    placed = tile_place.reshape(view_count, gz_count, gy_count, -1)
    slot_count = placed.shape[-1]
    entries = view_count * slot_count
    group = lax.dynamic_index_in_dim(placed, my_gz, 1, keepdims=False)
    group = group.transpose(1, 0, 2).reshape(gy_count, entries)
    destination = group // positions
    dest_gy = destination % gy_count
    ahead = (destination // gy_count - my_gz) % gz_count
    view = jnp.arange(entries) // slot_count % chunk
    cell = (ahead * chunk + view) * positions + group % positions
    own_dest = lax.dynamic_index_in_dim(dest_gy, my_gy, 0, keepdims=True)
    sends = own_dest == jnp.arange(gy_count)[:, None]
    takes = dest_gy == my_gy
    number = jnp.broadcast_to(jnp.arange(entries)[None, :], takes.shape)
    chosen = jnp.stack([sends, takes])
    value = jnp.stack([number, cell])
    upto = (jnp.arange(entries)[:, None] <= jnp.arange(entries)[None, :]).astype(jnp.bfloat16)
    rank = jnp.dot(chosen.astype(jnp.bfloat16), upto, preferred_element_type=jnp.float32)
    rank = jnp.where(chosen, rank.astype(jnp.int32) - 1, -1)

    def table(first, lanes):
        hit = rank[..., None, :] == first + jnp.arange(lanes)[:, None]
        return jnp.sum(jnp.where(hit, value[..., None, :], 0), axis=-1).astype(jnp.int32)

    ends = [
        jnp.sum(takes[:, : c * chunk * slot_count], axis=-1).astype(jnp.int32)
        for c in range(chunks + 1)
    ]
    return table, jnp.stack(ends)


def most_slots(tile_place, positions):
    gy_count = lax.axis_size("gy")
    route_count = lax.axis_size(("gz", "gy"))
    dest_gy = (tile_place // positions) % gy_count
    dest_gy = dest_gy.reshape(tile_place.shape[0], route_count, 1, -1)
    return jnp.max(jnp.sum(dest_gy == jnp.arange(gy_count)[:, None], axis=(0, 3)))


def pack_kernel(source, tiles, outgoing):
    partners, lanes = outgoing.shape[:2]

    def one(partner, carry):
        for lane in range(lanes):
            outgoing[partner, lane] = tiles[source[partner, lane]]
        return carry

    lax.fori_loop(0, partners, one, 0)


def join_kernel(chunk, ends, cell, late_cell, arrived, late, *blocks_and_total):
    blocks, total = blocks_and_total[:-1], blocks_and_total[-1]
    partners, usual = arrived.shape[:2]
    step = 16

    def clear(index, carry):
        total[pl.ds(index * step, step)] = jnp.zeros((step,) + total.shape[1:], total.dtype)
        return carry

    lax.fori_loop(0, total.shape[0] // step, clear, 0)

    def add(cells, tiles, partner, lane):
        place = cells[partner, lane]
        total[place] = add_rounded(total[place], tiles[partner, lane])

    for partner in range(partners):
        first, last = ends[chunk, partner], ends[chunk + 1, partner]

        def add_usual(lane, carry):
            add(cell, arrived, partner, lane)
            return carry

        def add_late(lane, carry):
            add(late_cell, late, partner, lane - usual)
            return carry

        lax.fori_loop(jnp.minimum(first, usual), jnp.minimum(last, usual), add_usual, 0)
        lax.fori_loop(jnp.maximum(first, usual), jnp.maximum(last, usual), add_late, 0)
    start = 0
    for block in blocks:
        block[...] = total[start : start + block.shape[0]]
        start += block.shape[0]


def pack(source, tiles):
    return pl.pallas_call(
        pack_kernel,
        out_shape=jax.ShapeDtypeStruct(source.shape + tiles.shape[1:], tiles.dtype),
        in_specs=[smem, vmem],
        out_specs=vmem,
        compiler_params=pltpu.CompilerParams(vmem_limit_bytes=32 << 20),
        name="pack",
    )(source, tiles)


def join(chunk, ends, cell, late_cell, arrived, late, devices, cells):
    tile = arrived.shape[2:]
    half = devices // 2
    sizes = [cells] * half + [cells // 2] * 2 + [cells] * (half - 1)
    return pl.pallas_call(
        functools.partial(join_kernel, chunk),
        out_shape=[jax.ShapeDtypeStruct((size,) + tile, arrived.dtype) for size in sizes],
        in_specs=[smem, smem, smem, vmem, vmem],
        out_specs=[vmem] * len(sizes),
        scratch_shapes=[pltpu.VMEM((devices * cells,) + tile, arrived.dtype)],
        compiler_params=pltpu.CompilerParams(vmem_limit_bytes=32 << 20),
        name="join",
    )(ends, cell, late_cell, arrived, late)


def unwritten(shape, dtype):
    return pl.pallas_call(
        lambda out: None,
        out_shape=jax.ShapeDtypeStruct(shape, dtype),
        out_specs=pl.BlockSpec(memory_space=pl.ANY),
        name="unwritten",
    )()


def exchange(value):
    return lax.all_to_all(value, "gy", split_axis=0, concat_axis=0, tiled=True)


def add_rounded(left, right):
    return (left.astype(jnp.float32) + right.astype(jnp.float32)).astype(left.dtype)


def ring_step(upward, downward):
    devices = lax.axis_size("gz")
    up = [(i, (i + 1) % devices) for i in range(devices)]
    down = [(j, i) for i, j in up]
    return lax.ppermute(upward, "gz", up), lax.ppermute(downward, "gz", down)


def ring_sum(blocks):
    devices = len(blocks) - 1
    half = devices // 2
    from_below, from_above = ring_step(blocks[half], blocks[half + 1])
    middle = blocks[half].shape[0]
    for ahead in range(half - 1, 0, -1):
        upward, downward = blocks[ahead], blocks[devices - ahead + 1]
        if ahead == half - 1:
            upward = jnp.concatenate([add_rounded(upward[:middle], from_below), upward[middle:]])
            downward = jnp.concatenate(
                [downward[:middle], add_rounded(downward[middle:], from_above)]
            )
        else:
            upward = add_rounded(upward, from_below)
            downward = add_rounded(downward, from_above)
        from_below, from_above = ring_step(upward, downward)
    return (
        blocks[0].astype(jnp.float32)
        + from_below.astype(jnp.float32)
        + from_above.astype(jnp.float32)
    )


def on_device(recorded, tile_place, psf, estimate):
    view_count = recorded.shape[0]
    tile_depth, tile_rows = recorded.shape[2:4]
    depth, rows, cols = estimate.shape
    per_row = rows // tile_rows
    positions = depth // tile_depth * per_row
    area = depth * rows
    radius = (psf.shape[2] - 1) // 2
    side = 16
    tall, wide = depth + 2 * side, rows + 2 * side
    chunks = 2
    chunk = view_count // chunks
    gz_count, gy_count = lax.axis_size("gz"), lax.axis_size("gy")
    tiles = recorded.reshape(-1, tile_depth * tile_rows, cols)
    lanes = gz_count * capacity * view_count
    usual = min(usual_slots, lanes)
    own = estimate.astype(jnp.bfloat16)
    own_rows = neighbours(own, own, "gy")
    table, ends = slot_tables(tile_place, positions, chunks, usual)
    usual_table = table(0, usual)

    def late_exchange():
        late_table = table(usual, lanes - usual)
        return exchange(pack(late_table[0], tiles)), late_table[1]

    def no_exchange():
        shape = (gy_count, lanes - usual)
        return unwritten(shape + tiles.shape[1:], tiles.dtype), jnp.zeros(shape, jnp.int32)

    late, late_cell = lax.cond(
        most_slots(tile_place, positions) > usual, late_exchange, no_exchange
    )
    usual_table, late_cell = lax.optimization_barrier((usual_table, late_cell))
    outgoing = pack(usual_table[0], tiles)
    outgoing, psf = lax.optimization_barrier((outgoing, psf))
    own_rows, _ = lax.optimization_barrier((own_rows, psf))
    arrived = exchange(outgoing)

    kernels = psf / jnp.sum(psf, axis=-1, keepdims=True)
    line = jnp.arange(area)
    place, inside = line // (tile_depth * tile_rows), line % (tile_depth * tile_rows)
    line_depth = place // per_row * tile_depth + inside // tile_rows
    line_row = place % per_row * tile_rows + inside % tile_rows
    reach = radius - side
    depth_taps = taps_table(kernels[:, 0], jnp.arange(tall)[:, None] - line_depth[None, :] + reach)
    row_taps = taps_table(kernels[:, 1], jnp.arange(wide)[:, None] - line_row[None, :] + reach)
    sheets = []
    for v in range(0, view_count, chunk):
        down = depth_taps[v : v + chunk].transpose(1, 0, 2).reshape(tall, 1, chunk * area)
        across = row_taps[v : v + chunk].transpose(1, 0, 2).reshape(1, wide, chunk * area)
        sheet = (down * across).astype(jnp.bfloat16)
        sheets.append(sheet.reshape(tall * wide, chunk * area))
    above, below = order_sides(*own_rows, "gy")
    own = jnp.concatenate([above, own, below], axis=1)
    above, below = order_sides(*neighbours(own, own, "gz"), "gz")
    own = jnp.concatenate([above, own, below], axis=0)
    own = own.reshape(tall * wide, cols)
    column = jnp.concatenate(
        [jnp.arange(cols), jnp.arange(-side, 0), jnp.arange(cols, cols + side)]
        + [jnp.full(cols - 2 * side, -cols)]
    )
    offset = column[:, None] - jnp.arange(cols)[None, :]
    col_taps = taps_table(kernels[:, 2], radius + offset).astype(jnp.bfloat16)
    first, second = column_sides(own, side)
    arrived, first, second = lax.optimization_barrier((arrived, first, second))
    blocks = [
        join(c, ends, usual_table[1], late_cell, arrived, late, gz_count, chunk * positions)
        for c in range(chunks)
    ]
    back_kernels, _ = lax.optimization_barrier((kernels[:, 2], blocks[-1][0]))
    col_taps_back = taps_table(back_kernels, radius - offset).astype(jnp.bfloat16)
    first, second, _ = lax.optimization_barrier((first, second, blocks[-1][0]))
    field = with_columns(own, first, second)
    blurred = []
    for c in range(chunks):
        swept = lax.dot_general(
            sheets[c], field, (((0,), (0,)), ((), ())), preferred_element_type=jnp.float32
        )
        swept = swept.astype(jnp.bfloat16).reshape(chunk, area, -1)
        blurred.append(
            jnp.einsum(
                "vac,vck->vak",
                swept,
                col_taps[c * chunk : (c + 1) * chunk],
                preferred_element_type=jnp.float32,
            )
        )
    joined = [ring_sum(blocks[c]) for c in range(chunks)]
    total = jnp.zeros((tall * wide, cols), jnp.float32)
    for c in range(chunks):
        views = slice(c * chunk, (c + 1) * chunk)
        ratio = joined[c].reshape(chunk, area, cols) / (blurred[c] + background_level)
        ratio = ratio.astype(jnp.bfloat16).reshape(chunk * area, cols)
        ratio = with_columns(ratio, *column_sides(ratio, side)).reshape(chunk, area, -1)
        spread = jnp.einsum(
            "vac,vck->vak", ratio, col_taps_back[views], preferred_element_type=jnp.float32
        )
        spread = spread.astype(jnp.bfloat16).reshape(chunk * area, cols)
        total = total + jnp.dot(sheets[c], spread, preferred_element_type=jnp.float32)
    total = total.reshape(tall, wide, cols)
    first, second = neighbours(
        total[side + depth :].astype(jnp.float16), total[:side].astype(jnp.float16), "gz"
    )
    total = total[side : side + depth] + first.astype(jnp.float32) + second.astype(jnp.float32)
    first, second = neighbours(
        total[:, side + rows :].astype(jnp.float16), total[:, :side].astype(jnp.float16), "gy"
    )
    result = total[:, side : side + rows] + first.astype(jnp.float32) + second.astype(jnp.float32)
    return estimate * result / view_count


def solution(mesh):
    placed = (P(None, ("gz", "gy"), None, None, "gx"), P(), P(), P("gz", "gy", "gx"))
    return jax.shard_map(
        on_device, mesh=mesh, in_specs=placed, out_specs=P("gz", "gy", "gx"), check_vma=False
    )
```
